256 devices in a mesh: img: 32 (over z, x), tp: 8 (over y, core).
Axes of the slice: x: 4, y: 4, z: 8, core: 2. Of those that a mesh axis runs over, the one named last changes fastest.
Arguments:
- vision_tokens: bfloat16 [16384, 1280], P('img')
- inter_feats: bfloat16 [16384, 2560], P('img'), may hold values from -6 to 6
- fc1_weight: bfloat16 [1280, 2560], P(None, 'tp'), may hold values from -0.15625 to 0.15625
- fc2_weight: bfloat16 [2560, 1280], P('tp'), may hold values from -0.125 to 0.125
- proj_weight: bfloat16 [3840, 8192], P('img', 'tp'), may hold values from -0.09375 to 0.09375
- kv_weight: bfloat16 [8192, 2048], P('tp'), may hold values from -0.0625 to 0.0625
- tile_counts: int32 [128], replicated, may hold values from 1 to 4
- owner_map: int32 [128], replicated, may hold values from 0 to 31, as said below
- decode_hidden: bfloat16 [128, 8192], P(None, 'img'), may hold values from -6 to 6
- query_weight: bfloat16 [8192, 8192], P('img', 'tp'), may hold values from -0.0625 to 0.0625
Outputs:
- vision_states: bfloat16 [16384, 8192], P('img', 'tp')
- kv_cache: bfloat16 [256, 128, 2048], P('img', None, 'tp')
- attended: bfloat16 [256, 8192], P('img', 'tp')
The draws below stay inside these ranges and needn't reach their ends.
Inputs may be any that keep to these rules, and one draw needn't show every extreme that they name: `owner_map`: among the 16 requests b * 16 to (b + 1) * 16 - 1 no owner is named more than 1 times. Every owner is named at least once and at most 8 times, and one owner exactly 8 times.
All inputs are finite; a program needn't handle non-finite values.
Results may differ from the reference program's by a relative error of at most 0.013.
Values may be sent and summed in bfloat16 or wider, within the bound.
No kernel may reach another device: no remote copies, remote signals or barrier semaphores. Data moves between devices by JAX's collectives and lax.ppermute only.
A program may use at most 64 MiB of HBM per device.

```python
import math
import jax
import jax.numpy as jnp
from jax import lax

D = 8192
QH = 64
KVH = 8
HD = 128
ENC = 1280
HID = 2560
PIN = 3840
TILES = 4
TILE_TOK = 32
REQ = 128
GROUPS = 8
BLOCK = 16
CAP = 8
TOK = 16384
INTER = 2560
N_IMG = 32


def scaled_field(subkey, lowest, highest):
    row_key, column_key = jax.random.split(subkey)
    row_scale = jnp.exp(jax.random.uniform(row_key, (TOK, 1), minval=math.log(lowest), maxval=math.log(highest)))
    column_scale = jnp.exp(jax.random.uniform(column_key, (1, ENC), minval=math.log(lowest), maxval=math.log(highest)))
    return row_scale * column_scale


def draw_vision_tokens(key, part):
    key = jax.random.fold_in(key, 11)
    scale_key, base_key = jax.random.split(key, 2)
    values = jax.random.normal(base_key, (TOK, ENC)) * scaled_field(scale_key, 0.3, 3.0)
    return values.astype(jnp.bfloat16)


def shuffled(subkey):
    return jax.random.permutation(subkey, BLOCK)


def draw_owner_map(key, part):
    key = jax.random.fold_in(key, 23)
    label_key, extra_key, order_key, place_key = jax.random.split(key, 4)
    spare = (N_IMG - 1) * (CAP - 1)
    candidates = 1 + jnp.arange(spare, dtype=jnp.int32) // (CAP - 1)
    extras = jax.random.permutation(extra_key, candidates)[:REQ - CAP - (N_IMG - 1)]
    listed = jnp.concatenate([jnp.zeros((CAP,), jnp.int32), jnp.arange(1, N_IMG, dtype=jnp.int32), extras.astype(jnp.int32)])
    ordered = jnp.sort(listed)
    labels = jax.random.permutation(label_key, N_IMG).astype(jnp.int32)
    owners = labels[ordered]
    spots = jnp.arange(REQ, dtype=jnp.int32)
    block_order = jax.random.permutation(order_key, GROUPS).astype(jnp.int32)
    placings = jax.vmap(shuffled)(jax.random.split(place_key, GROUPS)).astype(jnp.int32)
    blocks = block_order[spots % GROUPS]
    positions = placings[blocks, spots // GROUPS]
    return jnp.zeros((REQ,), jnp.int32).at[blocks * BLOCK + positions].set(owners)


def set_ends(array, stream_key, low, top_value):
    longest = array.shape.index(max(array.shape))
    spots = []
    for shift in (0, 1):
        where = [jax.random.randint(jax.random.fold_in(stream_key, axis), (), 0, length) for axis, length in enumerate(array.shape)]
        where[longest] = (where[longest] + shift) % array.shape[longest]
        spots.append(tuple(where))
    return array.at[spots[0]].set(low).at[spots[1]].set(top_value)


def levels(rng, extent, pieces, low, high):
    loudness, own = 1.0, jax.random.fold_in(rng, 6)
    for axis_at, parts in pieces:
        heights = jnp.exp(jax.random.uniform(jax.random.fold_in(own, axis_at), (parts,), jnp.float32, low / len(pieces), high / len(pieces)))
        loudness = loudness * jnp.repeat(heights, extent[axis_at] // parts).reshape([-1 if axis == axis_at else 1 for axis in range(len(extent))])
    return loudness


def gaussian(rng, shape, scale, limit, shards=(), held_as=jnp.bfloat16):
    array = jax.random.normal(rng, shape, jnp.float32) * scale
    if len(shards) > 0:
        array = levels(rng, shape, shards, -0.22, 0.18) * array
    return jnp.clip(array, min=-limit, max=limit).astype(held_as)


def setup_inputs(seed: int = 0) -> dict:
    splits = jax.random.split(jax.random.key(seed), 11)
    return {
        "vision_tokens": draw_vision_tokens(jax.random.fold_in(splits[10], 71), 0),
        "inter_feats": gaussian(splits[1], (TOK, INTER), 1.0, 6.0, ((0, 32),)),
        "fc1_weight": gaussian(splits[2], (ENC, HID), ENC ** -0.5, 0.15625, ((1, 8),)),
        "fc2_weight": gaussian(splits[3], (HID, ENC), HID ** -0.5, 0.125, ((0, 8),)),
        "proj_weight": gaussian(splits[4], (PIN, D), PIN ** -0.5, 0.09375, ((0, 32), (1, 8))),
        "kv_weight": gaussian(splits[5], (D, KVH * 2 * HD), D ** -0.5, 0.0625, ((0, 8),)),
        "tile_counts": set_ends(jax.random.randint(splits[6], (REQ,), 1, TILES + 1), jax.random.fold_in(splits[6], 1), 1, TILES).astype(jnp.int32),
        "owner_map": draw_owner_map(jax.random.fold_in(splits[10], 71), 0),
        "decode_hidden": gaussian(splits[8], (REQ, D), 1.0, 6.0, ((1, 32),)),
        "query_weight": gaussian(splits[9], (D, QH * HD), D ** -0.5, 0.0625, ((0, 32), (1, 8))),
    }


def reference(vision_tokens, inter_feats, fc1_weight, fc2_weight, proj_weight, kv_weight, tile_counts, owner_map, decode_hidden, query_weight):
    tokens_wide = vision_tokens.astype(jnp.float32)
    center = tokens_wide - lax.optimization_barrier(jnp.mean(tokens_wide, -1, keepdims=True))
    spread = lax.optimization_barrier(jnp.mean(center * center, -1, keepdims=True))
    normed = (center * lax.rsqrt(spread + 1e-05)).astype(jnp.bfloat16)
    hidden = jax.nn.gelu(jnp.dot(normed, fc1_weight, preferred_element_type=jnp.float32), approximate=False).astype(jnp.bfloat16)
    encoded = (tokens_wide + jnp.dot(hidden, fc2_weight, preferred_element_type=jnp.float32)).astype(jnp.bfloat16)
    features = jnp.concatenate([encoded, inter_feats], 1)
    vision_states = jnp.dot(features, proj_weight, preferred_element_type=jnp.float32).astype(jnp.bfloat16)
    paired = jnp.dot(vision_states, kv_weight, preferred_element_type=jnp.float32).reshape(TOK, KVH, 2, HD)
    keys_raw = paired[:, :, 0, :]
    keys_normed = keys_raw * lax.rsqrt(lax.optimization_barrier(jnp.mean(keys_raw * keys_raw, -1, keepdims=True)) + 1e-06)
    kv_tokens = jnp.stack([keys_normed, paired[:, :, 1, :]], 2).astype(jnp.bfloat16)
    kv_width = KVH * 2 * HD
    tiled = kv_tokens.reshape(TILES, REQ, TILE_TOK, kv_width)
    tile_live = jnp.arange(TILES, dtype=jnp.int32)[:, None] < tile_counts[None, :]
    tiled = jnp.where(tile_live[:, :, None, None], tiled, jnp.zeros((), jnp.bfloat16))
    per_request = jnp.transpose(tiled, (1, 0, 2, 3)).reshape(REQ, TILES * TILE_TOK, kv_width)
    request_ids = jnp.arange(REQ, dtype=jnp.int32)
    same_owner = owner_map[:, None] == owner_map[None, :]
    slot_rank = lax.optimization_barrier(jnp.sum((same_owner & (request_ids[None, :] < request_ids[:, None])).astype(jnp.int32), 1))
    flat_slot = (owner_map * CAP + slot_rank).astype(jnp.int32)
    kv_cache = jnp.zeros((N_IMG * CAP, TILES * TILE_TOK, kv_width), jnp.bfloat16).at[flat_slot].set(per_request)
    queries = jnp.dot(decode_hidden, query_weight, preferred_element_type=jnp.float32).reshape(REQ, QH, HD)
    queries = (queries * lax.rsqrt(lax.optimization_barrier(jnp.mean(queries * queries, -1, keepdims=True)) + 1e-06)).astype(jnp.bfloat16)
    grouped = queries.reshape(REQ, KVH, QH // KVH, HD).astype(jnp.float32)
    stored = per_request.reshape(REQ, TILES * TILE_TOK, KVH, 2, HD).astype(jnp.float32)
    scores = jnp.einsum('rhgd,rlhd->rhgl', grouped, stored[:, :, :, 0, :]) / math.sqrt(HD)
    key_live = (jnp.arange(TILES * TILE_TOK, dtype=jnp.int32) // TILE_TOK)[None, :] < tile_counts[:, None]
    weights = jnp.where(key_live[:, None, None, :], jnp.exp(scores), 0.0).astype(jnp.bfloat16)
    weights_wide = weights.astype(jnp.float32)
    totals = lax.optimization_barrier(jnp.sum(weights_wide, -1))
    numerator = jnp.einsum('rhgl,rlhd->rhgd', weights_wide, stored[:, :, :, 1, :])
    attn_rows = (numerator / totals[..., None]).reshape(REQ, QH * HD).astype(jnp.bfloat16)
    attended = jnp.zeros((N_IMG * CAP, QH * HD), jnp.bfloat16).at[flat_slot].set(attn_rows)
    return (vision_states, kv_cache, attended)
```

```python
import math

import jax
import jax.numpy as jnp
from jax import lax
from jax.sharding import Mesh, PartitionSpec as P

QH = 64
KVH = 8
HD = 128
TILES = 4
NZ, NX, NY, NC = 8, 4, 4, 2
NIMG = NZ * NX
BLOCK = 16
CAP = 8
KVW = 2 * HD
EARLY = 128
BF = jnp.bfloat16
F32 = jnp.float32


def shift(value, axis, step):
    n = lax.axis_size(axis)
    return lax.ppermute(value, axis, [(i, (i + step) % n) for i in range(n)])


def dot(a, b):
    return jnp.dot(a, b, preferred_element_type=F32)


def pick(array, index, axis=0):
    return lax.dynamic_index_in_dim(array, index, axis, keepdims=False)


def place(buffer, value, index, axis):
    return lax.dynamic_update_index_in_dim(buffer, value, index, axis)


def rms_scale(values, epsilon):
    return values * lax.rsqrt(jnp.mean(values * values, -1, keepdims=True) + epsilon)


def ring_z(own, zi, cut, buffer, axis, split):
    buffer = place(buffer, own, zi, axis)
    up, down = own, own
    for step in range(1, NZ // 2):
        up, down = shift(up, "z", 1), shift(down, "z", -1)
        buffer = place(buffer, up, (zi - step) % NZ, axis)
        buffer = place(buffer, down, (zi + step) % NZ, axis)
    first, second = split(up, down, cut)
    far = jnp.concatenate([shift(first, "z", 1), shift(second, "z", -1)], 0)
    return place(buffer, far, (zi + NZ // 2) % NZ, axis)


def halves(up, down, cut):
    return up[:cut], down[cut:]


def per_device(
    vision_tokens,
    inter_feats,
    fc1_weight,
    fc2_weight,
    proj_weight,
    kv_weight,
    tile_counts,
    owner_map,
    decode_hidden,
    query_weight,
):
    zi, xi = lax.axis_index("z"), lax.axis_index("x")
    yi, ci = lax.axis_index("y"), lax.axis_index("c")
    img_index = zi * NX + xi
    rows = vision_tokens.shape[0]
    shard = proj_weight.shape[0]
    tile_len = rows // BLOCK
    requests = tile_counts.shape[0]

    late = proj_weight[:, EARLY:]
    late_block = ring_z(late, zi, 64, jnp.zeros((NZ,) + late.shape, BF), 0, halves)
    late_block = late_block.reshape(NZ * shard, -1)

    product = dot(proj_weight, kv_weight).reshape(shard, NY, NC, KVW)
    product = jnp.transpose(product, (2, 1, 0, 3))
    swapped = shift(pick(product, 1 - ci).astype(BF), "c", 1)
    half_sum = pick(product, ci) + swapped.astype(F32)
    joined = pick(half_sum, yi)
    for step in (1, -1, 2):
        joined = joined + shift(pick(half_sum, (yi + step) % NY).astype(BF), "y", step).astype(F32)
    early = jnp.concatenate([joined.astype(BF), proj_weight[:, :EARLY]], 1)

    from_left, from_right, from_far = shift(early, "x", 1), shift(early, "x", -1), shift(early, "x", 2)
    early_block = jnp.zeros((NX,) + early.shape, BF)
    for step, value in ((0, early), (-1, from_left), (1, from_right), (2, from_far)):
        early_block = place(early_block, value, (xi + step) % NX, 0)
    early_all = ring_z(
        early_block, zi, NX // 2, jnp.zeros((NX, NZ) + early.shape, BF), 1, halves
    ).reshape(NX, 2, NZ * shard // 2, -1)

    left, right = shift(late_block, "x", 1), shift(late_block, "x", -1)
    mid = NZ * shard // 2
    far_first, far_second = shift(left[:mid], "x", 1), shift(right[mid:], "x", -1)

    tokens_wide = vision_tokens.astype(F32)
    center = tokens_wide - jnp.mean(tokens_wide, -1, keepdims=True)
    spread = jnp.mean(center * center, -1, keepdims=True)
    normed = (center * lax.rsqrt(spread + 1e-05)).astype(BF)
    hidden = jax.nn.gelu(dot(normed, fc1_weight), approximate=False).astype(BF)
    partial_value = dot(hidden, fc2_weight)
    width = partial_value.shape[1]
    quarter = rows // (NC * NY)
    by_place = partial_value.reshape(NC, NY, quarter, width)
    swapped = shift(pick(by_place, 1 - ci).astype(BF), "c", 1)
    half_sum = pick(by_place, ci) + swapped.astype(F32)
    total = pick(half_sum, yi)
    for step in (1, -1, 2):
        total = total + shift(pick(half_sum, (yi + step) % NY).astype(BF), "y", step).astype(F32)
    tokens_here = pick(pick(tokens_wide.reshape(NC, NY, quarter, width), ci), yi)
    piece = (tokens_here + total).astype(BF)
    pieces = place(jnp.zeros((NY,) + piece.shape, BF), piece, yi, 0)
    for step in (1, -1, 2):
        pieces = place(pieces, shift(piece, "y", step), (yi - step) % NY, 0)
    other = shift(pieces, "c", 1)
    encoded = jnp.zeros((NC,) + pieces.shape, BF)
    encoded = place(place(encoded, pieces, ci, 0), other, 1 - ci, 0).reshape(rows, width)

    features = jnp.concatenate([encoded, inter_feats], 1)
    feats = jnp.transpose(
        features.reshape(rows, 2, NZ // 2, NX, shard), (3, 1, 0, 2, 4)
    ).reshape(NX, 2, rows, mid)

    early_out = jnp.zeros((rows, early.shape[1]), F32)
    for x in range(NX):
        for h in range(2):
            early_out = early_out + dot(feats[x, h], early_all[x, h])

    def late_dot(step, first, second):
        here = pick(feats, (xi + step) % NX)
        return dot(here[0], first) + dot(here[1], second)

    late_out = late_dot(0, late_block[:mid], late_block[mid:])
    late_out = late_out + late_dot(-1, left[:mid], left[mid:])
    late_out = late_out + late_dot(1, right[:mid], right[mid:])
    late_out = late_out + late_dot(2, far_first, far_second)
    vision_states = jnp.concatenate([early_out[:, KVW:].astype(BF), late_out.astype(BF)], 1)

    request_ids = jnp.arange(requests, dtype=jnp.int32)
    same_owner = owner_map[:, None] == owner_map[None, :]
    earlier = same_owner & (request_ids[None, :] < request_ids[:, None])
    slot_rank = jnp.sum(earlier.astype(jnp.int32), 1)
    slot_match = (owner_map[None, :] == img_index) & (
        slot_rank[None, :] == jnp.arange(CAP, dtype=jnp.int32)[:, None]
    )
    present = jnp.any(slot_match, 1)
    request_of = jnp.sum(jnp.where(slot_match, request_ids[None, :], 0), 1)
    count_of = jnp.where(
        present, jnp.sum(jnp.where(slot_match, tile_counts[None, :], 0), 1), 1
    )

    slot_row = jnp.arange(NIMG * CAP, dtype=jnp.int32)
    row_owner = (slot_row // CAP) % NZ * NX + slot_row // (CAP * NZ)
    slot_hot = (owner_map[None, :] == row_owner[:, None]) & (
        slot_rank[None, :] == (slot_row % CAP)[:, None]
    )
    slot_hidden = dot(slot_hot.astype(BF), decode_hidden).astype(BF)
    queries = dot(slot_hidden, query_weight)
    queries = lax.psum_scatter(queries, "x", scatter_dimension=0, tiled=True)
    queries = lax.psum_scatter(queries, "z", scatter_dimension=0, tiled=True)
    slot_queries = rms_scale(queries.reshape(CAP, -1, HD), 1e-06).astype(BF)

    keys = rms_scale(early_out[:, :HD], 1e-06)
    kv_tokens = jnp.concatenate([keys, early_out[:, HD:KVW]], 1).astype(BF)
    tile_here, block_here = img_index // NZ, img_index % NZ
    owners_here = lax.dynamic_slice_in_dim(owner_map, block_here * BLOCK, BLOCK)
    counts_here = lax.dynamic_slice_in_dim(tile_counts, block_here * BLOCK, BLOCK)
    send_row = jnp.arange(NIMG * tile_len, dtype=jnp.int32)
    token_row = jnp.arange(rows, dtype=jnp.int32)
    owner_of_token = jnp.repeat(jnp.where(tile_here < counts_here, owners_here, -1), tile_len)
    send_hot = (
        (send_row // tile_len)[:, None] * tile_len + (send_row % tile_len)[:, None]
        == (owner_of_token * tile_len + token_row % tile_len)[None, :]
    ).astype(BF)
    outgoing = dot(send_hot, kv_tokens).astype(BF).reshape(NIMG, tile_len, KVW)
    arrived = lax.all_to_all(outgoing, ("z", "x"), 0, 0, tiled=True)
    arrived = arrived.reshape(NIMG * tile_len, KVW)
    groups = NIMG // TILES
    cache_row = jnp.arange(CAP * TILES * tile_len, dtype=jnp.int32)
    cache_tile = cache_row // tile_len % TILES
    source = cache_tile * groups + jnp.repeat(request_of // BLOCK, TILES * tile_len)
    wanted = jnp.where(
        jnp.repeat(present, TILES * tile_len), source * tile_len + cache_row % tile_len, -1
    )
    cache_hot = (wanted[:, None] == send_row[None, :]).astype(BF)
    kv_cache = dot(cache_hot, arrived).astype(BF).reshape(CAP, TILES * tile_len, KVW)

    scores = jnp.einsum(
        "cgd,cld->cgl", slot_queries, kv_cache[:, :, :HD], preferred_element_type=F32
    ) / math.sqrt(HD)
    key_live = (jnp.arange(TILES * tile_len, dtype=jnp.int32) // tile_len)[None, :] < count_of[
        :, None
    ]
    weights = jnp.where(key_live[:, None, :], jnp.exp(scores), 0.0).astype(BF)
    totals = jnp.sum(weights, -1, dtype=F32)
    numerator = jnp.einsum(
        "cgl,cld->cgd", weights, kv_cache[:, :, HD:], preferred_element_type=F32
    )
    attended = (numerator / totals[..., None]).reshape(CAP, -1).astype(BF)
    attended = jnp.where(present[:, None], attended, jnp.zeros((), BF))
    return (vision_states, kv_cache, attended)


def solution(mesh):
    img, tp = ("z", "x"), ("y", "c")
    fine = Mesh(mesh.devices.reshape(NZ, NX, NY, NC), img + tp)
    return jax.shard_map(
        per_device,
        mesh=fine,
        in_specs=(
            P(img, None),
            P(img, None),
            P(None, tp),
            P(tp, None),
            P(img, tp),
            P(tp, None),
            P(),
            P(),
            P(None, img),
            P(img, tp),
        ),
        out_specs=(P(img, tp), P(img, None, tp), P(img, tp)),
        check_vma=False,
    )
```

```python
import functools
import math

import jax
import jax.numpy as jnp
from jax import lax
from jax.experimental import pallas as pl
from jax.experimental.pallas import tpu as pltpu
from jax.sharding import Mesh, PartitionSpec as P

QH = 64
KVH = 8
HD = 128
TILES = 4
NZ, NX, NY, NC = 8, 4, 4, 2
NIMG = NZ * NX
BLOCK = 16
CAP = 8
GROUP = QH // KVH
KVW = 2 * HD
SIDE = 256
BF = jnp.bfloat16
F32 = jnp.float32
I32 = jnp.int32
VMEM_LIMIT = 48 * 2**20


def shift(value, axis, step):
    n = lax.axis_size(axis)
    return lax.ppermute(value, axis, [(i, (i + step) % n) for i in range(n)])


def dot(a, b):
    return jnp.dot(a, b, preferred_element_type=F32)


def pick(array, index, axis=0):
    return lax.dynamic_index_in_dim(array, index, axis, keepdims=False)


def place(buffer, value, index, axis):
    return lax.dynamic_update_index_in_dim(buffer, value, index, axis)


def rms_scale(values, epsilon):
    return values * lax.rsqrt(jnp.mean(values * values, -1, keepdims=True) + epsilon)


def shape(dims, dtype=BF):
    return jax.ShapeDtypeStruct(dims, dtype)


def call(body, grid, ins, outs, out_shape, scalars, operands, flops, nbytes):
    return pl.pallas_call(
        body,
        grid_spec=pltpu.PrefetchScalarGridSpec(
            num_scalar_prefetch=len(scalars), grid=grid, in_specs=ins, out_specs=outs
        ),
        out_shape=out_shape,
        compiler_params=pltpu.CompilerParams(vmem_limit_bytes=VMEM_LIMIT),
        cost_estimate=pl.CostEstimate(flops=flops, bytes_accessed=nbytes, transcendentals=0),
    )(*scalars, *operands)


def fold_body(core, proj, kv, send, keep):
    product = dot(proj[...], kv[...])
    first = pl.program_id(0) == 0

    @pl.when(first)
    def _():
        send[0] = product.astype(BF)

    @pl.when(jnp.logical_not(first))
    def _():
        keep[0] = product


def fold_weights(core, proj, kv):
    rows, depth = proj.shape
    return call(
        fold_body,
        (2, NY),
        [
            pl.BlockSpec((rows, depth), lambda h, y, c: (0, 0)),
            pl.BlockSpec(
                (depth, KVW), lambda h, y, c: (0, 2 * y + jnp.where(h == 0, 1 - c[0], c[0]))
            ),
        ],
        [
            pl.BlockSpec((1, rows, KVW), lambda h, y, c: (jnp.where(h == 0, y, NY - 1), 0, 0)),
            pl.BlockSpec((1, rows, KVW), lambda h, y, c: (jnp.where(h == 0, 0, y), 0, 0)),
        ],
        [shape((NY, rows, KVW)), shape((NY, rows, KVW), F32)],
        [core],
        [proj, kv],
        2 * rows * depth * kv.shape[1],
        2 * kv.size,
    )


def layer_body(core, tokens, fc1, fc2, send, keep):
    wide = tokens[...].astype(F32)
    center = wide - jnp.mean(wide, -1, keepdims=True)
    spread = jnp.mean(center * center, -1, keepdims=True)
    normed = (center * lax.rsqrt(spread + 1e-05)).astype(BF)
    value = dot(normed, fc1[...])
    hidden = (0.5 * value * (1.0 + lax.erf(value * math.sqrt(0.5)))).astype(BF)
    partial = dot(hidden, fc2[...])
    first = pl.program_id(0) == 0

    @pl.when(first)
    def _():
        send[...] = partial.astype(BF)

    @pl.when(jnp.logical_not(first))
    def _():
        keep[...] = partial


def layer(core, tokens, fc1, fc2):
    rows, width = tokens.shape
    block = rows // 4
    return call(
        layer_body,
        (2, 2),
        [
            pl.BlockSpec(
                (block, width), lambda h, k, c: (2 * jnp.where(h == 0, 1 - c[0], c[0]) + k, 0)
            ),
            pl.BlockSpec(fc1.shape, lambda h, k, c: (0, 0)),
            pl.BlockSpec(fc2.shape, lambda h, k, c: (0, 0)),
        ],
        [
            pl.BlockSpec((block, width), lambda h, k, c: (jnp.where(h == 0, k, 1), 0)),
            pl.BlockSpec((block, width), lambda h, k, c: (jnp.where(h == 0, 0, k), 0)),
        ],
        [shape((rows // 2, width)), shape((rows // 2, width), F32)],
        [core],
        [tokens, fc1, fc2],
        4 * rows * width * fc1.shape[1],
        4 * tokens.size,
    )


def regroup_body(shard, encoded, inter, out):
    features = jnp.concatenate([encoded[...], inter[...]], 1)
    for x in range(NX):
        starts = [(z * NX + x) * shard for z in range(NZ)]
        out[x] = jnp.concatenate([features[:, s : s + shard] for s in starts], 1)


def regroup(encoded, inter, shard):
    rows = encoded.shape[0]
    block = rows // 4
    return call(
        functools.partial(regroup_body, shard),
        (4,),
        [
            pl.BlockSpec((block, encoded.shape[1]), lambda i: (i, 0)),
            pl.BlockSpec((block, inter.shape[1]), lambda i: (i, 0)),
        ],
        pl.BlockSpec((NX, block, NZ * shard), lambda i: (0, i, 0)),
        shape((NX, rows, NZ * shard)),
        [],
        [encoded, inter],
        0,
        4 * (encoded.size + inter.size),
    )


def relay_body(tile_len, owners, encoded, inter, weight, out):
    step = pl.program_id(0)
    split = encoded.shape[1]
    paired = dot(encoded[...], weight[:split]) + dot(inter[...], weight[split:])
    keys = rms_scale(paired[:, :HD], 1e-06)
    tokens = jnp.concatenate([keys, paired[:, HD:]], 1).astype(BF)

    @pl.when(step == 0)
    def _():
        out[...] = jnp.zeros_like(out)

    count = encoded.shape[0] // tile_len
    for q in range(count):
        owner = owners[step * count + q]

        @pl.when(owner >= 0)
        def _(q=q, owner=owner):
            start = pl.multiple_of(owner * tile_len, tile_len)
            out[pl.ds(start, tile_len), :] = tokens[q * tile_len : (q + 1) * tile_len]


def relay_rows(owners, encoded, inter, weight):
    rows = encoded.shape[0]
    tile_len = rows // BLOCK
    block = rows // 4
    return call(
        functools.partial(relay_body, tile_len),
        (4,),
        [
            pl.BlockSpec((block, encoded.shape[1]), lambda i, o: (i, 0)),
            pl.BlockSpec((block, inter.shape[1]), lambda i, o: (i, 0)),
            pl.BlockSpec(weight.shape, lambda i, o: (0, 0)),
        ],
        pl.BlockSpec((NIMG * tile_len, KVW), lambda i, o: (0, 0)),
        shape((NIMG * tile_len, KVW)),
        [owners],
        [encoded, inter, weight],
        2 * rows * weight.size,
        2 * (encoded.size + inter.size + weight.size),
    )


def decode_body(tile_len, info, arrived, queries, cache, attended):
    groups = NIMG // TILES
    length = TILES * tile_len
    results = []
    for c in range(CAP):
        block, present, count = info[0, c], info[1, c] > 0, info[2, c]
        for j in range(TILES):
            start = pl.multiple_of((j * groups + block) * tile_len, tile_len)
            rows = arrived[pl.ds(start, tile_len), :]
            cache[c, j * tile_len : (j + 1) * tile_len, :] = jnp.where(
                present, rows, jnp.zeros_like(rows)
            )
        keys, values = cache[c, :, :HD], cache[c, :, HD:]
        scores = lax.dot_general(
            queries[c], keys, (((1,), (1,)), ((), ())), preferred_element_type=F32
        ) / math.sqrt(HD)
        tile = lax.broadcasted_iota(I32, (GROUP, length), 1) // tile_len
        weights = jnp.where(tile < count, jnp.exp(scores), 0.0).astype(BF)
        totals = jnp.sum(weights.astype(F32), -1, keepdims=True)
        result = dot(weights, values) / totals
        results.append(jnp.where(present, result, jnp.zeros_like(result)))
    for g in range(GROUP):
        column = jnp.concatenate([r[g : g + 1] for r in results], 0)
        attended[:, g * HD : (g + 1) * HD] = column.astype(BF)


def decode(info, arrived, queries):
    tile_len = arrived.shape[0] // NIMG
    length = TILES * tile_len
    return call(
        functools.partial(decode_body, tile_len),
        (1,),
        [
            pl.BlockSpec(arrived.shape, lambda i, s: (0, 0)),
            pl.BlockSpec(queries.shape, lambda i, s: (0, 0, 0)),
        ],
        [
            pl.BlockSpec((CAP, length, KVW), lambda i, s: (0, 0, 0)),
            pl.BlockSpec((CAP, GROUP * HD), lambda i, s: (0, 0)),
        ],
        [shape((CAP, length, KVW)), shape((CAP, GROUP * HD))],
        [info],
        [arrived, queries],
        4 * CAP * GROUP * length * HD,
        4 * arrived.size,
    )


def near_body(x, own, left, right, feats_own, feats_left, feats_right, out):
    total = dot(feats_own[0], own[...])
    total = total + dot(feats_left[0], left[...])
    out[...] = total + dot(feats_right[0], right[...])


def near_sum(x, own, left, right, feats):
    rows, depth = feats.shape[1:]
    width = own.shape[1]
    block = rows // 4
    whole = pl.BlockSpec((depth, width), lambda i, x: (0, 0))

    def part(step):
        return pl.BlockSpec((1, block, depth), lambda i, x: ((x[0] + step) % NX, i, 0))

    return call(
        near_body,
        (4,),
        [whole, whole, whole, part(0), part(NX - 1), part(1)],
        pl.BlockSpec((block, width), lambda i, x: (i, 0)),
        shape((rows, width), F32),
        [x],
        [own, left, right, feats, feats, feats],
        6 * rows * depth * width,
        6 * depth * (rows + width),
    )


def last_body(x, near, far_first, far_second, feats, encoded, inter, side, out):
    mid = far_first.shape[0]
    split = encoded.shape[1]
    width = side.shape[1]
    total = near[...] + dot(feats[0, :, :mid], far_first[...])
    total = total + dot(feats[0, :, mid:], far_second[...])
    aside = dot(encoded[...], side[:split]) + dot(inter[...], side[split:])
    out[:, :width] = aside.astype(BF)
    out[:, width:] = total.astype(BF)


def last_sum(x, near, far_first, far_second, feats, encoded, inter, side):
    rows, depth = feats.shape[1:]
    width = near.shape[1]
    block = rows // 4
    total = width + side.shape[1]
    half = pl.BlockSpec(far_first.shape, lambda i, x: (0, 0))
    return call(
        last_body,
        (4,),
        [
            pl.BlockSpec((block, width), lambda i, x: (i, 0)),
            half,
            half,
            pl.BlockSpec((1, block, depth), lambda i, x: ((x[0] + 2) % NX, i, 0)),
            pl.BlockSpec((block, encoded.shape[1]), lambda i, x: (i, 0)),
            pl.BlockSpec((block, inter.shape[1]), lambda i, x: (i, 0)),
            pl.BlockSpec(side.shape, lambda i, x: (0, 0)),
        ],
        pl.BlockSpec((block, total), lambda i, x: (i, 0)),
        shape((rows, total)),
        [x],
        [near, far_first, far_second, feats, encoded, inter, side],
        2 * rows * (depth * width + side.size),
        2 * (side.size + depth * width + 2 * rows * total),
    )


def per_device(
    vision_tokens,
    inter_feats,
    fc1_weight,
    fc2_weight,
    proj_weight,
    kv_weight,
    tile_counts,
    owner_map,
    decode_hidden,
    query_weight,
):
    zi, xi = lax.axis_index("z"), lax.axis_index("x")
    yi, ci = lax.axis_index("y"), lax.axis_index("c")
    img_index = zi * NX + xi
    core = ci.astype(I32)[None]
    column = xi.astype(I32)[None]
    rows, width = vision_tokens.shape
    shard = proj_weight.shape[0]
    tile_len = rows // BLOCK
    requests = tile_counts.shape[0]

    send, keep = fold_weights(core, proj_weight, kv_weight)
    half_sum = shift(send, "c", 1).astype(F32) + keep
    joined = pick(half_sum, yi)
    for step in (1, -1, 2):
        joined = joined + shift(pick(half_sum, (yi + step) % NY).astype(BF), "y", step).astype(F32)
    early = jnp.concatenate([joined.astype(BF), proj_weight[:, :SIDE]], 1)

    block = jnp.zeros((NX,) + early.shape, BF)
    for step, value in (
        (0, early),
        (-1, shift(early, "x", 1)),
        (1, shift(early, "x", -1)),
        (2, shift(early, "x", 2)),
    ):
        block = place(block, value, (xi + step) % NX, 0)
    block = block.reshape(NX * shard, -1)
    folded = lax.all_gather(block[:, :KVW], "z", axis=0, tiled=True)
    side = lax.all_gather(block[:, KVW:], "z", axis=0, tiled=True)

    late = proj_weight[:, SIDE:]
    own = place(jnp.zeros((NZ,) + late.shape, BF), late, zi, 0)
    up, down = late, late
    for step in range(1, NZ // 2):
        up, down = shift(up, "z", 1), shift(down, "z", -1)
        own = place(own, up, (zi - step) % NZ, 0)
        own = place(own, down, (zi + step) % NZ, 0)
    cut = 64
    far = jnp.concatenate([shift(up[:cut], "z", 1), shift(down[cut:], "z", -1)], 0)
    own = place(own, far, (zi + NZ // 2) % NZ, 0).reshape(NZ * shard, -1)
    left, right = shift(own, "x", 1), shift(own, "x", -1)
    mid = NZ * shard // 2
    far_first, far_second = shift(left[:mid], "x", 1), shift(right[mid:], "x", -1)

    send, keep = layer(core, vision_tokens, fc1_weight, fc2_weight)
    half_sum = shift(send, "c", 1).astype(F32) + keep
    quarter = rows // (NC * NY)
    half_sum = half_sum.reshape(NY, quarter, width)
    total = pick(half_sum, yi)
    for step in (1, -1, 2):
        total = total + shift(pick(half_sum, (yi + step) % NY).astype(BF), "y", step).astype(F32)
    tokens_here = pick(vision_tokens.reshape(NC * NY, quarter, width), ci * NY + yi)
    piece = (tokens_here.astype(F32) + total).astype(BF)
    pieces = place(jnp.zeros((NY,) + piece.shape, BF), piece, yi, 0)
    for step in (1, -1, 2):
        pieces = place(pieces, shift(piece, "y", step), (yi - step) % NY, 0)
    pieces = pieces.reshape(rows // 2, width)
    other = shift(pieces, "c", 1)
    encoded = jnp.concatenate(
        [jnp.where(ci == 0, pieces, other), jnp.where(ci == 0, other, pieces)], 0
    )

    request_ids = jnp.arange(requests, dtype=I32)
    same_owner = owner_map[:, None] == owner_map[None, :]
    earlier = same_owner & (request_ids[None, :] < request_ids[:, None])
    slot_rank = jnp.sum(earlier.astype(I32), 1)
    slot_match = (owner_map[None, :] == img_index) & (
        slot_rank[None, :] == jnp.arange(CAP, dtype=I32)[:, None]
    )
    present = jnp.any(slot_match, 1)
    request_of = jnp.sum(jnp.where(slot_match, request_ids[None, :], 0), 1)
    count_of = jnp.where(
        present, jnp.sum(jnp.where(slot_match, tile_counts[None, :], 0), 1), 1
    )
    info = jnp.stack([request_of // BLOCK, present.astype(I32), count_of])

    slot_row = jnp.arange(NIMG * CAP, dtype=I32)
    slot_hot = (owner_map[None, :] == (slot_row // CAP)[:, None]) & (
        slot_rank[None, :] == (slot_row % CAP)[:, None]
    )
    slot_hidden = dot(slot_hot.astype(BF), decode_hidden).astype(BF)
    partial = dot(slot_hidden, query_weight).astype(BF).reshape(NIMG, CAP, GROUP * HD)
    partial = lax.all_to_all(partial, ("z", "x"), 0, 0, tiled=True)
    queries = jnp.sum(partial.astype(F32), 0)
    slot_queries = rms_scale(queries.reshape(CAP, GROUP, HD), 1e-06).astype(BF)

    tile_here, block_here = img_index // NZ, img_index % NZ
    owners_here = lax.dynamic_slice_in_dim(owner_map, block_here * BLOCK, BLOCK)
    counts_here = lax.dynamic_slice_in_dim(tile_counts, block_here * BLOCK, BLOCK)
    targets = jnp.where(tile_here < counts_here, owners_here, -1)
    outgoing = relay_rows(targets, encoded, inter_feats, folded)
    arrived = lax.all_to_all(
        outgoing.reshape(NIMG, tile_len, KVW), ("z", "x"), 0, 0, tiled=True
    )
    kv_cache, attended = decode(info, arrived.reshape(NIMG * tile_len, KVW), slot_queries)

    feats = regroup(encoded, inter_feats, shard)
    near = near_sum(column, own, left, right, feats)
    vision_states = last_sum(
        column, near, far_first, far_second, feats, encoded, inter_feats, side
    )
    return (vision_states, kv_cache, attended)


def solution(mesh):
    img, tp = ("z", "x"), ("y", "c")
    fine = Mesh(mesh.devices.reshape(NZ, NX, NY, NC), img + tp)
    return jax.shard_map(
        per_device,
        mesh=fine,
        in_specs=(
            P(img, None),
            P(img, None),
            P(None, tp),
            P(tp, None),
            P(img, tp),
            P(tp, None),
            P(),
            P(),
            P(None, img),
            P(img, tp),
        ),
        out_specs=(P(img, tp), P(img, None, tp), P(img, tp)),
        check_vma=False,
    )
```

```python
import functools
import math

import jax
import jax.numpy as jnp
from jax import lax
from jax.experimental import pallas as pl
from jax.experimental.pallas import tpu as pltpu
from jax.sharding import Mesh, PartitionSpec as P

QH = 64
KVH = 8
HD = 128
TILES = 4
NZ, NX, NY, NC = 8, 4, 4, 2
NIMG = NZ * NX
BLOCK = 16
CAP = 8
GROUP = QH // KVH
KVW = 2 * HD
BF = jnp.bfloat16
F32 = jnp.float32
I32 = jnp.int32
VMEM_LIMIT = 14 * 2**20
COST = 1
LAST_COST = 10**8
HOPS = (0, -1, 1, 2)
HOPS = (0, -1, 1, 2)


def shift(value, axis, step):
    n = lax.axis_size(axis)
    return lax.ppermute(value, axis, [(i, (i + step) % n) for i in range(n)])


def tick(array):
    return array.reshape(-1, array.shape[-1])[:8, :HD]


def dot(a, b):
    return jnp.dot(a, b, preferred_element_type=F32)


def pick(array, index, axis=0):
    return lax.dynamic_index_in_dim(array, index, axis, keepdims=False)


def place(buffer, value, index, axis):
    return lax.dynamic_update_index_in_dim(buffer, value, index, axis)


def rms_scale(values, epsilon):
    return values * lax.rsqrt(jnp.mean(values * values, -1, keepdims=True) + epsilon)


def shape(dims, dtype=BF):
    return jax.ShapeDtypeStruct(dims, dtype)


def call(body, out_shape, scalars, operands, after=(), scratch=(), space=pltpu.VMEM, cost=COST):
    lead = len(scalars) + len(operands)

    def kernel(*refs):
        body(*refs[:lead], *refs[lead + len(after) :])

    smem, vmem = (pl.BlockSpec(memory_space=space) for space in (pltpu.SMEM, pltpu.VMEM))
    several = isinstance(out_shape, (list, tuple))
    return pl.pallas_call(
        kernel,
        in_specs=[smem] * len(scalars)
        + [pl.BlockSpec(memory_space=space)] * len(operands)
        + [pl.BlockSpec(memory_space=pl.ANY)] * len(after),
        out_specs=[vmem] * len(out_shape) if several else vmem,
        out_shape=out_shape,
        scratch_shapes=scratch,
        compiler_params=pltpu.CompilerParams(vmem_limit_bytes=VMEM_LIMIT),
        cost_estimate=pl.CostEstimate(flops=cost, bytes_accessed=cost, transcendentals=0),
    )(*scalars, *operands, *after)


def fold_body(core, proj, kv, send, keep):
    for here in range(NC):

        @pl.when(core[0] == here)
        def _(here=here):
            for y in range(NY):
                other, mine = (2 * y + 1 - here) * KVW, (2 * y + here) * KVW
                send[y] = dot(proj[...], kv[:, other : other + KVW]).astype(BF)
                keep[y] = dot(proj[...], kv[:, mine : mine + KVW])


def fold_weights(core, proj, kv):
    dims = (NY, proj.shape[0], KVW)
    return call(fold_body, [shape(dims), shape(dims, F32)], [core], [proj, kv])


def half_body(y, swapped, keep, up, down, across, own):
    for step, out in ((1, up), (NY - 1, down), (2, across)):
        place = (y[0] + step) % NY
        out[...] = (swapped[place].astype(F32) + keep[place]).astype(BF)
    own[...] = swapped[y[0]].astype(F32) + keep[y[0]]


def half_sums(y, swapped, keep, after=()):
    dims = keep.shape[1:]
    outs = [shape(dims)] * 3 + [shape(dims, F32)]
    return call(half_body, outs, [y], [swapped, keep], after)


def join_body(own, up, down, across, out):
    total = own[...] + up[...].astype(F32) + down[...].astype(F32) + across[...].astype(F32)
    out[...] = total.astype(BF)


def join(own, parts, after):
    return call(join_body, shape(own.shape), [], [own, *parts], after)


def block_body(x, own, left, right, far, out):
    for step, value in zip(HOPS, (own, left, right, far)):
        out[(x[0] + step) % NX] = value[...]


def in_order(x, parts, after):
    return call(block_body, shape((NX,) + parts[0].shape), [x], parts, after)


def layer_body(core, tokens, fc1, fc2, send, keep):
    half = tokens.shape[0] // NC

    def rows(which):
        wide = tokens[pl.ds(pl.multiple_of(which * half, half), half), :].astype(F32)
        center = wide - jnp.mean(wide, -1, keepdims=True)
        spread = jnp.mean(center * center, -1, keepdims=True)
        normed = (center * lax.rsqrt(spread + 1e-05)).astype(BF)
        value = lax.dot_general(
            normed, fc1[...], (((1,), (1,)), ((), ())), preferred_element_type=F32
        )
        hidden = (0.5 * value * (1.0 + lax.erf(value * math.sqrt(0.5)))).astype(BF)
        return dot(hidden, fc2[...])

    send[...] = rows(1 - core[0]).astype(BF).reshape(send.shape)
    keep[...] = rows(core[0]).reshape(keep.shape)


def layer(core, tokens, fc1, fc2, after):
    dims = (NY, tokens.shape[0] // (NC * NY), tokens.shape[1])
    return call(layer_body, [shape(dims), shape(dims, F32)], [core], [tokens, fc1, fc2], after)


def piece_body(place, own, up, down, across, tokens, out):
    total = own[...] + up[...].astype(F32) + down[...].astype(F32) + across[...].astype(F32)
    rows = own.shape[0]
    here = tokens[pl.ds(pl.multiple_of(place[0] * rows, rows), rows), :]
    out[...] = (here.astype(F32) + total).astype(BF)


def encoded_piece(place, own, parts, tokens, after):
    return call(piece_body, shape(own.shape), [place], [own, *parts, tokens], after)


def regroup_body(shard, encoded, inter, out):
    part = encoded.shape[0] // 4
    for r in range(0, encoded.shape[0], part):
        features = jnp.concatenate([encoded[r : r + part], inter[r : r + part]], 1)
        for x in range(NX):
            for half in range(2):
                places = range(half * NZ // 2, (half + 1) * NZ // 2)
                starts = [(z * NX + x) * shard for z in places]
                out[2 * x + half, r : r + part] = jnp.concatenate(
                    [features[:, s : s + shard] for s in starts], 1
                )


def regroup(encoded, inter, shard):
    dims = (2 * NX, encoded.shape[0], NZ // 2 * shard)
    return call(functools.partial(regroup_body, shard), shape(dims), [], [encoded, inter])


def relay_body(tile_len, owners, encoded, inter, weight, out, features, table, total, sems):
    split = encoded.shape[1]
    steps = weight.shape[0] // split
    copies = []
    for k in range(steps):
        rows = pl.ds(k * split, split)
        source = encoded if k == 0 else inter.at[:, pl.ds((k - 1) * split, split)]
        copies.append(pltpu.make_async_copy(source, features.at[k], sems.at[2 * k]))
        copies.append(pltpu.make_async_copy(weight.at[rows], table.at[k], sems.at[2 * k + 1]))
    for copy in copies:
        copy.start()
    out[...] = jnp.zeros_like(out)
    for k in range(steps):
        copies[2 * k].wait()
        copies[2 * k + 1].wait()
        if k == 0:
            total[...] = dot(features[k], table[k])
        else:
            total[...] += dot(features[k], table[k])
    keys = rms_scale(total[:, :HD], 1e-06)
    tokens = jnp.concatenate([keys, total[:, HD:]], 1).astype(BF)
    for q in range(BLOCK):
        owner = owners[q]

        @pl.when(owner >= 0)
        def _(q=q, owner=owner):
            out[owner] = tokens[q * tile_len : (q + 1) * tile_len]


def relay_rows(owners, encoded, inter, weight, after):
    rows, split = encoded.shape
    tile_len = rows // BLOCK
    width = weight.shape[1]
    steps = weight.shape[0] // split
    return call(
        functools.partial(relay_body, tile_len),
        shape((NIMG, tile_len, KVW)),
        [owners],
        [encoded, inter, weight],
        after,
        scratch=[
            pltpu.VMEM((steps, rows, split), BF),
            pltpu.VMEM((steps, split, width), BF),
            pltpu.VMEM((rows, width), F32),
            pltpu.SemaphoreType.DMA((2 * steps,)),
        ],
        space=pltpu.HBM,
    )


def query_body(hot, hidden, weight, out):
    out[...] = dot(dot(hot[...], hidden[...]).astype(BF), weight[...]).astype(BF).reshape(out.shape)


def query_part(hot, hidden, weight, after):
    out = shape((NIMG, CAP, weight.shape[1]))
    return call(query_body, out, [], [hot, hidden, weight], after)


def normed_body(parts, out):
    total = jnp.sum(parts[...].astype(F32), 0)
    for g in range(GROUP):
        out[g] = rms_scale(total[:, g * HD : (g + 1) * HD], 1e-06)


def normed_queries(parts):
    return call(normed_body, shape((GROUP, CAP, HD), F32), [], [parts])


def decode_body(info, arrived, queries, cache, attended):
    groups = NIMG // TILES
    tile_len = arrived.shape[1]
    length = TILES * tile_len
    results = []
    for c in range(CAP):
        block, present, count = info[0, c], info[1, c] > 0, info[2, c]
        for j in range(TILES):
            rows = arrived[j * groups + block]
            cache[c, j * tile_len : (j + 1) * tile_len, :] = jnp.where(
                present, rows, jnp.zeros_like(rows)
            )
        keys, values = cache[c, :, :HD], cache[c, :, HD:]
        heads = jnp.concatenate([queries[g, c : c + 1] for g in range(GROUP)], 0).astype(BF)
        scores = lax.dot_general(
            heads, keys, (((1,), (1,)), ((), ())), preferred_element_type=F32
        ) / math.sqrt(HD)
        tile = lax.broadcasted_iota(I32, (GROUP, length), 1) // tile_len
        weights = jnp.where(tile < count, jnp.exp(scores), 0.0).astype(BF)
        totals = jnp.sum(weights.astype(F32), -1, keepdims=True)
        result = dot(weights, values) / totals
        results.append(jnp.where(present, result, jnp.zeros_like(result)))
    for g in range(GROUP):
        column = jnp.concatenate([r[g : g + 1] for r in results], 0)
        attended[:, g * HD : (g + 1) * HD] = column.astype(BF)


def decode(info, arrived, queries):
    outs = [shape((CAP, TILES * arrived.shape[1], KVW)), shape((CAP, GROUP * HD))]
    return call(decode_body, outs, [info], [arrived, queries])


def near_body(x, feats, own, left, right, out):
    mid = own.shape[0] // 2
    here, before, after = ((x[0] + step) % NX * 2 for step in HOPS[:3])
    out[...] = dot(feats[here], own[:mid]) + dot(feats[here + 1], own[mid:])
    out[...] += dot(feats[before], left[...]) + dot(feats[after + 1], right[...])


def near_sum(x, feats, weights):
    dims = (feats.shape[1], weights[0].shape[1])
    return call(near_body, shape(dims, F32), [x], [feats, *weights])


def last_body(x, near, feats, left, right, first, second, out, places, sems):
    copies = [
        pltpu.make_async_copy(w, places.at[k], sems.at[k])
        for k, w in enumerate((left, right, first, second))
    ]
    for copy in copies:
        copy.start()
    before, after, across = ((x[0] + step) % NX * 2 for step in HOPS[1:])
    total = near[...]
    for k, row in enumerate((before + 1, after, across, across + 1)):
        copies[k].wait()
        total = total + dot(feats[row], places[k])
    out[...] = total.astype(BF)


def last_sum(x, near, feats, weights):
    dims = near.shape
    smem, vmem, hbm = (
        pl.BlockSpec(memory_space=space) for space in (pltpu.SMEM, pltpu.VMEM, pltpu.HBM)
    )
    return pl.pallas_call(
        last_body,
        in_specs=[smem, vmem, vmem] + [hbm] * 4,
        out_specs=vmem,
        out_shape=shape(dims),
        scratch_shapes=[
            pltpu.VMEM((4,) + weights[0].shape, BF),
            pltpu.SemaphoreType.DMA((4,)),
        ],
        compiler_params=pltpu.CompilerParams(vmem_limit_bytes=VMEM_LIMIT),
        cost_estimate=pl.CostEstimate(
            flops=LAST_COST, bytes_accessed=LAST_COST, transcendentals=0
        ),
    )(x, near, feats, *weights)


def per_device(
    vision_tokens,
    inter_feats,
    fc1_weight,
    fc2_weight,
    proj_weight,
    kv_weight,
    tile_counts,
    owner_map,
    decode_hidden,
    query_weight,
):
    zi, xi = lax.axis_index("z"), lax.axis_index("x")
    yi, ci = lax.axis_index("y"), lax.axis_index("c")
    img_index = zi * NX + xi
    core = ci.astype(I32)[None]
    column = xi.astype(I32)[None]
    there = yi.astype(I32)[None]
    rows, width = vision_tokens.shape
    shard = proj_weight.shape[0]
    tile_len = rows // BLOCK
    requests = tile_counts.shape[0]

    late = lax.all_gather(proj_weight, "z", axis=0, tiled=True)
    mid = late.shape[0] // 2
    left_first, right_second = shift(late[:mid], "x", 1), shift(late[mid:], "x", -1)
    left_second, right_first = shift(late[mid:], "x", 1), shift(late[:mid], "x", -1)
    far = [shift(left_first, "x", 1), shift(right_second, "x", -1)]

    fold_send, fold_keep = fold_weights(core, proj_weight, kv_weight)
    *fold_parts, fold_own = half_sums(there, shift(fold_send, "c", 1), fold_keep)

    send, keep = layer(core, vision_tokens, fc1_weight.T, fc2_weight, [tick(fold_send)])
    *parts, total = half_sums(there, shift(send, "c", 1), keep, [tick(fold_parts[0])])

    fold_parts = [shift(p, "y", step) for step, p in zip((1, -1, 2), fold_parts)]
    joined = join(fold_own, fold_parts, [tick(parts[0])])

    parts = [shift(p, "y", step) for step, p in zip((1, -1, 2), parts)]
    place_here = (ci * NY + yi).astype(I32)[None]
    piece = encoded_piece(place_here, total, parts, vision_tokens, [tick(joined)])
    pieces = place(jnp.zeros((NY,) + piece.shape, BF), piece, yi, 0)
    for step in (1, -1, 2):
        pieces = place(pieces, shift(piece, "y", step), (yi - step) % NY, 0)
    pieces = pieces.reshape(rows // 2, width)
    other = shift(pieces, "c", 1)
    encoded = jnp.concatenate(
        [jnp.where(ci == 0, pieces, other), jnp.where(ci == 0, other, pieces)], 0
    )

    block = [joined, *(shift(joined, "x", step) for step in (1, -1, 2))]
    block = in_order(column, block, [tick(late)]).reshape(NX * shard, -1)
    early = lax.all_gather(block, "z", axis=0, tiled=True)

    request_ids = jnp.arange(requests, dtype=I32)
    same_owner = owner_map[:, None] == owner_map[None, :]
    earlier = same_owner & (request_ids[None, :] < request_ids[:, None])
    slot_rank = jnp.sum(earlier.astype(I32), 1)
    slot_match = (owner_map[None, :] == img_index) & (
        slot_rank[None, :] == jnp.arange(CAP, dtype=I32)[:, None]
    )
    present = jnp.any(slot_match, 1)
    request_of = jnp.sum(jnp.where(slot_match, request_ids[None, :], 0), 1)
    count_of = jnp.where(
        present, jnp.sum(jnp.where(slot_match, tile_counts[None, :], 0), 1), 1
    )
    info = jnp.stack([request_of // BLOCK, present.astype(I32), count_of])

    slot_row = jnp.arange(NIMG * CAP, dtype=I32)
    slot_hot = (owner_map[None, :] == (slot_row // CAP)[:, None]) & (
        slot_rank[None, :] == (slot_row % CAP)[:, None]
    )
    partial = query_part(slot_hot.astype(BF), decode_hidden, query_weight, [tick(encoded)])
    queries = normed_queries(lax.all_to_all(partial, ("z", "x"), 0, 0, tiled=True))

    feats = regroup(encoded, inter_feats, shard)
    tile_here, block_here = img_index // NZ, img_index % NZ
    owners_here = lax.dynamic_slice_in_dim(owner_map, block_here * BLOCK, BLOCK)
    counts_here = lax.dynamic_slice_in_dim(tile_counts, block_here * BLOCK, BLOCK)
    targets = jnp.where(tile_here < counts_here, owners_here, -1)
    outgoing = relay_rows(
        targets, encoded, inter_feats, early, [tick(feats), queries]
    )
    arrived = lax.all_to_all(outgoing, ("z", "x"), 0, 0, tiled=True)
    kv_cache, attended = decode(info, arrived, queries)

    near = near_sum(column, feats, [late, left_first, right_second])
    vision_states = last_sum(column, near, feats, [left_second, right_first, *far])
    return (vision_states, kv_cache, attended)


def solution(mesh):
    img, tp = ("z", "x"), ("y", "c")
    fine = Mesh(mesh.devices.reshape(NZ, NX, NY, NC), img + tp)
    return jax.shard_map(
        per_device,
        mesh=fine,
        in_specs=(
            P(img, None),
            P(img, None),
            P(None, tp),
            P(tp, None),
            P(img, tp),
            P(tp, None),
            P(),
            P(),
            P(None, img),
            P(img, tp),
        ),
        out_specs=(P(img, tp), P(img, None, tp), P(img, tp)),
        check_vma=False,
    )
```

```python
import functools
import math

import jax
import jax.numpy as jnp
from jax import lax
from jax.experimental import pallas as pl
from jax.experimental.pallas import tpu as pltpu
from jax.sharding import Mesh, PartitionSpec as P

QH = 64
KVH = 8
HD = 128
TILES = 4
NZ, NX, NY, NC = 8, 4, 4, 2
NIMG = NZ * NX
BLOCK = 16
CAP = 8
GROUP = QH // KVH
KVW = 2 * HD
BF = jnp.bfloat16
F32 = jnp.float32
I32 = jnp.int32
VMEM_LIMIT = 14 * 2**20
COST = 1
FAR_COST = 10**9
RELAY_LIMIT = 56 * 2**20
HOPS = (0, -1, 1, 2)
HOPS = (0, -1, 1, 2)


def shift(value, axis, step):
    n = lax.axis_size(axis)
    return lax.ppermute(value, axis, [(i, (i + step) % n) for i in range(n)])


def tick(array):
    return array.reshape(-1, array.shape[-1])[:8, :HD]


def dot(a, b):
    return jnp.dot(a, b, preferred_element_type=F32)


def pick(array, index, axis=0):
    return lax.dynamic_index_in_dim(array, index, axis, keepdims=False)


def place(buffer, value, index, axis):
    return lax.dynamic_update_index_in_dim(buffer, value, index, axis)


def rms_scale(values, epsilon):
    return values * lax.rsqrt(jnp.mean(values * values, -1, keepdims=True) + epsilon)


def shape(dims, dtype=BF):
    return jax.ShapeDtypeStruct(dims, dtype)


def call(body, out_shape, scalars, operands, after=(), scratch=(), space=pltpu.VMEM, cost=COST):
    lead = len(scalars) + len(operands)

    def kernel(*refs):
        body(*refs[:lead], *refs[lead + len(after) :])

    smem, vmem = (pl.BlockSpec(memory_space=space) for space in (pltpu.SMEM, pltpu.VMEM))
    several = isinstance(out_shape, (list, tuple))
    return pl.pallas_call(
        kernel,
        in_specs=[smem] * len(scalars)
        + [pl.BlockSpec(memory_space=space)] * len(operands)
        + [pl.BlockSpec(memory_space=pl.ANY)] * len(after),
        out_specs=[vmem] * len(out_shape) if several else vmem,
        out_shape=out_shape,
        scratch_shapes=scratch,
        compiler_params=pltpu.CompilerParams(vmem_limit_bytes=VMEM_LIMIT),
        cost_estimate=pl.CostEstimate(flops=cost, bytes_accessed=cost, transcendentals=0),
    )(*scalars, *operands, *after)


def fold_body(core, proj, kv, send, keep):
    for here in range(NC):

        @pl.when(core[0] == here)
        def _(here=here):
            for y in range(NY):
                other, mine = (2 * y + 1 - here) * KVW, (2 * y + here) * KVW
                send[y] = dot(proj[...], kv[:, other : other + KVW]).astype(BF)
                keep[y] = dot(proj[...], kv[:, mine : mine + KVW])


def fold_weights(core, proj, kv, after):
    dims = (NY, proj.shape[0], KVW)
    return call(fold_body, [shape(dims), shape(dims, F32)], [core], [proj, kv], after)


def half_body(y, swapped, keep, up, down, across, own):
    for step, out in ((1, up), (NY - 1, down), (2, across)):
        place = (y[0] + step) % NY
        out[...] = (swapped[place].astype(F32) + keep[place]).astype(BF)
    own[...] = swapped[y[0]].astype(F32) + keep[y[0]]


def half_sums(y, swapped, keep, after=()):
    dims = keep.shape[1:]
    outs = [shape(dims)] * 3 + [shape(dims, F32)]
    return call(half_body, outs, [y], [swapped, keep], after)


def join_body(own, up, down, across, out):
    total = own[...] + up[...].astype(F32) + down[...].astype(F32) + across[...].astype(F32)
    out[...] = total.astype(BF)


def join(own, parts, after):
    return call(join_body, shape(own.shape), [], [own, *parts], after)


def block_body(x, own, left, right, far, out):
    for step, value in zip(HOPS, (own, left, right, far)):
        out[(x[0] + step) % NX] = value[...]


def in_order(x, parts, after):
    return call(block_body, shape((NX,) + parts[0].shape), [x], parts, after)


def layer_body(core, tokens, fc1, fc2, send, keep):
    half = tokens.shape[0] // NC

    def rows(which):
        wide = tokens[pl.ds(pl.multiple_of(which * half, half), half), :].astype(F32)
        center = wide - jnp.mean(wide, -1, keepdims=True)
        spread = jnp.mean(center * center, -1, keepdims=True)
        normed = (center * lax.rsqrt(spread + 1e-05)).astype(BF)
        value = lax.dot_general(
            normed, fc1[...], (((1,), (1,)), ((), ())), preferred_element_type=F32
        )
        hidden = (0.5 * value * (1.0 + lax.erf(value * math.sqrt(0.5)))).astype(BF)
        return dot(hidden, fc2[...])

    send[...] = rows(1 - core[0]).astype(BF).reshape(send.shape)
    keep[...] = rows(core[0]).reshape(keep.shape)


def layer(core, tokens, fc1, fc2):
    dims = (NY, tokens.shape[0] // (NC * NY), tokens.shape[1])
    return call(layer_body, [shape(dims), shape(dims, F32)], [core], [tokens, fc1, fc2])


def regroup_body(shard, encoded, inter, out):
    part = encoded.shape[0] // 4
    for r in range(0, encoded.shape[0], part):
        features = jnp.concatenate([encoded[r : r + part], inter[r : r + part]], 1)
        for x in range(NX):
            for half in range(2):
                places = range(half * NZ // 2, (half + 1) * NZ // 2)
                starts = [(z * NX + x) * shard for z in places]
                out[2 * x + half, r : r + part] = jnp.concatenate(
                    [features[:, s : s + shard] for s in starts], 1
                )


def regroup(encoded, inter, shard):
    dims = (2 * NX, encoded.shape[0], NZ // 2 * shard)
    return call(functools.partial(regroup_body, shard), shape(dims), [], [encoded, inter])


def relay_body(tile_len, owners, encoded, inter, weight, hot, hidden, query, out, features, table, total, sems):
    split = encoded.shape[1]
    steps = weight.shape[0] // split
    copies = []
    for k in range(steps):
        rows = pl.ds(k * split, split)
        source = encoded if k == 0 else inter.at[:, pl.ds((k - 1) * split, split)]
        copies.append(pltpu.make_async_copy(source, features.at[k], sems.at[2 * k]))
        copies.append(pltpu.make_async_copy(weight.at[rows], table.at[k], sems.at[2 * k + 1]))
    for copy in copies:
        copy.start()
    out[:, :tile_len, :] = jnp.zeros((NIMG, tile_len, KVW), BF)

    slots = dot(hot[...], hidden[...]).astype(BF)
    for p in range(GROUP * HD // (2 * KVW)):
        pair = [
            dot(slots, query[:, (2 * p + i) * KVW : (2 * p + i + 1) * KVW]).reshape(
                NIMG, CAP, KVW
            )
            for i in range(2)
        ]
        start = tile_len + 2 * CAP * p
        out[:, start : start + 2 * CAP, :] = jnp.concatenate(pair, 1).astype(BF)

    for k in range(steps):
        copies[2 * k].wait()
        copies[2 * k + 1].wait()
        if k == 0:
            total[...] = dot(features[k], table[k])
        else:
            total[...] += dot(features[k], table[k])
    keys = rms_scale(total[:, :HD], 1e-06)
    tokens = jnp.concatenate([keys, total[:, HD:]], 1).astype(BF)
    for q in range(BLOCK):
        owner = owners[q]

        @pl.when(owner >= 0)
        def _(q=q, owner=owner):
            out[owner, :tile_len, :] = tokens[q * tile_len : (q + 1) * tile_len]


def relay_rows(owners, encoded, inter, weight, hot, hidden, query, after):
    rows, split = encoded.shape
    tile_len = rows // BLOCK
    height = tile_len + CAP * GROUP * HD // KVW
    steps = weight.shape[0] // split
    smem, vmem, hbm = (
        pl.BlockSpec(memory_space=space) for space in (pltpu.SMEM, pltpu.VMEM, pl.ANY)
    )

    def body(*refs):
        relay_body(tile_len, *refs[:7], *refs[7 + len(after) :])

    return pl.pallas_call(
        body,
        in_specs=[smem] + [hbm] * 3 + [vmem] * 3 + [hbm] * len(after),
        out_specs=vmem,
        out_shape=shape((NIMG, height, KVW)),
        scratch_shapes=[
            pltpu.VMEM((steps, rows, split), BF),
            pltpu.VMEM((steps, split, KVW), BF),
            pltpu.VMEM((rows, KVW), F32),
            pltpu.SemaphoreType.DMA((2 * steps,)),
        ],
        compiler_params=pltpu.CompilerParams(vmem_limit_bytes=RELAY_LIMIT),
        cost_estimate=pl.CostEstimate(flops=COST, bytes_accessed=COST, transcendentals=0),
    )(owners, encoded, inter, weight, hot, hidden, query, *after)


def decode_body(tile_len, info, arrived, cache, attended):
    groups = NIMG // TILES
    length = TILES * tile_len
    sums = jnp.sum(arrived[:, tile_len:, :].astype(F32), 0)
    queries = [
        rms_scale(sums[:, h * HD : (h + 1) * HD], 1e-06).reshape(-1, CAP, HD) for h in range(2)
    ]
    results = []
    for c in range(CAP):
        block, present, count = info[0, c], info[1, c] > 0, info[2, c]
        for j in range(TILES):
            rows = arrived[j * groups + block, :tile_len, :]
            cache[c, j * tile_len : (j + 1) * tile_len, :] = jnp.where(
                present, rows, jnp.zeros_like(rows)
            )
        keys, values = cache[c, :, :HD], cache[c, :, HD:]
        heads = jnp.concatenate([q[:, c, :] for q in queries], 0).astype(BF)
        scores = lax.dot_general(
            heads, keys, (((1,), (1,)), ((), ())), preferred_element_type=F32
        ) / math.sqrt(HD)
        tile = lax.broadcasted_iota(I32, (GROUP, length), 1) // tile_len
        weights = jnp.where(tile < count, jnp.exp(scores), 0.0).astype(BF)
        totals = jnp.sum(weights.astype(F32), -1, keepdims=True)
        result = dot(weights, values) / totals
        results.append(jnp.where(present, result, jnp.zeros_like(result)))
    for row in range(GROUP):
        head = row % (GROUP // 2) * 2 + row // (GROUP // 2)
        column = jnp.concatenate([r[row : row + 1] for r in results], 0)
        attended[:, head * HD : (head + 1) * HD] = column.astype(BF)


def decode(info, arrived, tile_len):
    outs = [shape((CAP, TILES * tile_len, KVW)), shape((CAP, GROUP * HD))]
    return call(functools.partial(decode_body, tile_len), outs, [info], [arrived])


def near_body(x, feats, own, left, right, out):
    mid = own.shape[0] // 2
    for step, weight in zip(HOPS, (own, left, right)):
        row = (x[0] + step) % NX * 2
        term = dot(feats[row], weight[:mid]) + dot(feats[row + 1], weight[mid:])
        if step == 0:
            out[...] = term
        else:
            out[...] += term


def near_sum(x, feats, weights):
    dims = (feats.shape[1], weights[0].shape[1])
    return call(near_body, shape(dims, F32), [x], [feats, *weights])


def far_body(x, feats, first, second, out):
    row = (x[0] + HOPS[-1]) % NX * 2
    out[...] = dot(feats[row], first[...]) + dot(feats[row + 1], second[...])


def far_sum(x, feats, weights):
    dims = (feats.shape[1], weights[0].shape[1])
    return call(far_body, shape(dims, F32), [x], [feats, *weights], cost=FAR_COST)


def last_body(near, rest, out):
    out[...] = (near[...] + rest[...]).astype(BF)


def last_sum(near, rest):
    return call(last_body, shape(near.shape), [], [near, rest])


def per_device(
    vision_tokens,
    inter_feats,
    fc1_weight,
    fc2_weight,
    proj_weight,
    kv_weight,
    tile_counts,
    owner_map,
    decode_hidden,
    query_weight,
):
    zi, xi = lax.axis_index("z"), lax.axis_index("x")
    yi, ci = lax.axis_index("y"), lax.axis_index("c")
    img_index = zi * NX + xi
    core = ci.astype(I32)[None]
    column = xi.astype(I32)[None]
    there = yi.astype(I32)[None]
    rows, width = vision_tokens.shape
    shard = proj_weight.shape[0]
    tile_len = rows // BLOCK
    requests = tile_counts.shape[0]

    late = lax.all_gather(proj_weight, "z", axis=0, tiled=True)
    left, right = shift(late, "x", 1), shift(late, "x", -1)
    mid = late.shape[0] // 2
    far = [shift(left[:mid], "x", 1), shift(right[mid:], "x", -1)]

    send, keep = layer(core, vision_tokens, fc1_weight.T, fc2_weight)
    swapped = shift(send, "c", 1)

    fold_send, fold_keep = fold_weights(core, proj_weight, kv_weight, [send])
    *fold_parts, fold_own = half_sums(there, shift(fold_send, "c", 1), fold_keep)
    fold_parts = [shift(p, "y", step) for step, p in zip((1, -1, 2), fold_parts)]

    request_ids = jnp.arange(requests, dtype=I32)
    same_owner = owner_map[:, None] == owner_map[None, :]
    earlier = same_owner & (request_ids[None, :] < request_ids[:, None])
    slot_rank = jnp.sum(earlier.astype(I32), 1)
    slot_match = (owner_map[None, :] == img_index) & (
        slot_rank[None, :] == jnp.arange(CAP, dtype=I32)[:, None]
    )
    present = jnp.any(slot_match, 1)
    request_of = jnp.sum(jnp.where(slot_match, request_ids[None, :], 0), 1)
    count_of = jnp.where(
        present, jnp.sum(jnp.where(slot_match, tile_counts[None, :], 0), 1), 1
    )
    info = jnp.stack([request_of // BLOCK, present.astype(I32), count_of])

    *parts, total = half_sums(there, swapped, keep)
    for step, part in zip((1, -1, 2), parts):
        total = total + shift(part, "y", step).astype(F32)
    quarter = rows // (NC * NY)
    tokens_here = pick(vision_tokens.reshape(NC * NY, quarter, width), ci * NY + yi)
    piece = (tokens_here.astype(F32) + total).astype(BF)
    pieces = place(jnp.zeros((NY,) + piece.shape, BF), piece, yi, 0)
    gathered = [shift(piece, "y", step) for step in (1, -1, 2)]
    for step, value in zip((1, -1, 2), gathered):
        pieces = place(pieces, value, (yi - step) % NY, 0)
    pieces = pieces.reshape(rows // 2, width)
    other = shift(pieces, "c", 1)
    encoded = jnp.concatenate(
        [jnp.where(ci == 0, pieces, other), jnp.where(ci == 0, other, pieces)], 0
    )

    joined = join(fold_own, fold_parts, [tick(v) for v in gathered])
    block = [joined, *(shift(joined, "x", step) for step in (1, -1, 2))]
    block = in_order(column, block, [tick(late)]).reshape(NX * shard, -1)
    early = lax.all_gather(block, "z", axis=0, tiled=True)

    slot_row = jnp.arange(NIMG * CAP, dtype=I32)
    slot_hot = (owner_map[None, :] == (slot_row // CAP)[:, None]) & (
        slot_rank[None, :] == (slot_row % CAP)[:, None]
    )
    feats = regroup(encoded, inter_feats, shard)
    tile_here, block_here = img_index // NZ, img_index % NZ
    owners_here = lax.dynamic_slice_in_dim(owner_map, block_here * BLOCK, BLOCK)
    counts_here = lax.dynamic_slice_in_dim(tile_counts, block_here * BLOCK, BLOCK)
    targets = jnp.where(tile_here < counts_here, owners_here, -1)
    outgoing = relay_rows(
        targets, encoded, inter_feats, early, slot_hot.astype(BF), decode_hidden, query_weight, [tick(feats)]
    )
    arrived = lax.all_to_all(outgoing, ("z", "x"), 0, 0, tiled=True)
    kv_cache, attended = decode(info, arrived, tile_len)

    near = near_sum(column, feats, [late, left, right])
    vision_states = last_sum(near, far_sum(column, feats, far))
    return (vision_states, kv_cache, attended)


def solution(mesh):
    img, tp = ("z", "x"), ("y", "c")
    fine = Mesh(mesh.devices.reshape(NZ, NX, NY, NC), img + tp)
    return jax.shard_map(
        per_device,
        mesh=fine,
        in_specs=(
            P(img, None),
            P(img, None),
            P(None, tp),
            P(tp, None),
            P(img, tp),
            P(tp, None),
            P(),
            P(),
            P(None, img),
            P(img, tp),
        ),
        out_specs=(P(img, tp), P(img, None, tp), P(img, tp)),
        check_vma=False,
    )
```

```python
import functools
import math

import jax
import jax.numpy as jnp
from jax import lax
from jax.experimental import pallas as pl
from jax.experimental.pallas import tpu as pltpu
from jax.sharding import Mesh, PartitionSpec as P

QH = 64
KVH = 8
HD = 128
TILES = 4
NZ, NX, NY, NC = 8, 4, 4, 2
NIMG = NZ * NX
BLOCK = 16
CAP = 8
GROUP = QH // KVH
KVW = 2 * HD
BF = jnp.bfloat16
F32 = jnp.float32
I32 = jnp.int32
VMEM_LIMIT = 14 * 2**20
COST = 1
LAST_COST = 10**9
RELAY_LIMIT = 56 * 2**20
HOPS = (0, -1, 1, 2)
HOPS = (0, -1, 1, 2)


def shift(value, axis, step):
    n = lax.axis_size(axis)
    return lax.ppermute(value, axis, [(i, (i + step) % n) for i in range(n)])


def tick(array):
    return array.reshape(-1, array.shape[-1])[:8, :HD]


def dot(a, b):
    return jnp.dot(a, b, preferred_element_type=F32)


def pick(array, index, axis=0):
    return lax.dynamic_index_in_dim(array, index, axis, keepdims=False)


def place(buffer, value, index, axis):
    return lax.dynamic_update_index_in_dim(buffer, value, index, axis)


def rms_scale(values, epsilon):
    return values * lax.rsqrt(jnp.mean(values * values, -1, keepdims=True) + epsilon)


def shape(dims, dtype=BF):
    return jax.ShapeDtypeStruct(dims, dtype)


def call(body, out_shape, scalars, operands, after=(), scratch=(), space=pltpu.VMEM, cost=COST):
    lead = len(scalars) + len(operands)

    def kernel(*refs):
        body(*refs[:lead], *refs[lead + len(after) :])

    smem, vmem = (pl.BlockSpec(memory_space=space) for space in (pltpu.SMEM, pltpu.VMEM))
    several = isinstance(out_shape, (list, tuple))
    return pl.pallas_call(
        kernel,
        in_specs=[smem] * len(scalars)
        + [pl.BlockSpec(memory_space=space)] * len(operands)
        + [pl.BlockSpec(memory_space=pl.ANY)] * len(after),
        out_specs=[vmem] * len(out_shape) if several else vmem,
        out_shape=out_shape,
        scratch_shapes=scratch,
        compiler_params=pltpu.CompilerParams(vmem_limit_bytes=VMEM_LIMIT),
        cost_estimate=pl.CostEstimate(flops=cost, bytes_accessed=cost, transcendentals=0),
    )(*scalars, *operands, *after)


def fold_body(core, proj, kv, send, keep):
    for here in range(NC):

        @pl.when(core[0] == here)
        def _(here=here):
            for y in range(NY):
                other, mine = (2 * y + 1 - here) * KVW, (2 * y + here) * KVW
                send[y] = dot(proj[...], kv[:, other : other + KVW]).astype(BF)
                keep[y] = dot(proj[...], kv[:, mine : mine + KVW])


def fold_weights(core, proj, kv, after):
    dims = (NY, proj.shape[0], KVW)
    return call(fold_body, [shape(dims), shape(dims, F32)], [core], [proj, kv], after)


def half_body(y, swapped, keep, up, down, across, own):
    for step, out in ((1, up), (NY - 1, down), (2, across)):
        place = (y[0] + step) % NY
        out[...] = (swapped[place].astype(F32) + keep[place]).astype(BF)
    own[...] = swapped[y[0]].astype(F32) + keep[y[0]]


def half_sums(y, swapped, keep, after=()):
    dims = keep.shape[1:]
    outs = [shape(dims)] * 3 + [shape(dims, F32)]
    return call(half_body, outs, [y], [swapped, keep], after)


def join_body(own, up, down, across, out):
    total = own[...] + up[...].astype(F32) + down[...].astype(F32) + across[...].astype(F32)
    out[...] = total.astype(BF)


def join(own, parts, after):
    return call(join_body, shape(own.shape), [], [own, *parts], after)


def block_body(x, own, left, right, far, out):
    for step, value in zip(HOPS, (own, left, right, far)):
        out[(x[0] + step) % NX] = value[...]


def pair_body(which, own, other, out):
    out[which[0]] = own[...]
    out[1 - which[0]] = other[...]


def pair(which, own, other):
    return call(pair_body, shape((NC,) + own.shape), [which], [own, other])


def in_order(x, parts, after):
    return call(block_body, shape((NX,) + parts[0].shape), [x], parts, after)


def layer_body(core, source, first, second, send, keep, tokens, fc1, fc2, sems):
    parts = 4
    pairs = []
    for ref, place in ((source, tokens), (first, fc1), (second, fc2)):
        rows = ref.shape[0] // parts
        pairs += [
            (ref.at[k * rows : (k + 1) * rows], place.at[k * rows : (k + 1) * rows])
            for k in range(parts)
        ]
    copies = [pltpu.make_async_copy(s, d, sems.at[i]) for i, (s, d) in enumerate(pairs)]
    for copy in copies:
        copy.start()
    for copy in copies:
        copy.wait()
    half = tokens.shape[0] // NC

    def rows(which):
        wide = tokens[pl.ds(pl.multiple_of(which * half, half), half), :].astype(F32)
        center = wide - jnp.mean(wide, -1, keepdims=True)
        spread = jnp.mean(center * center, -1, keepdims=True)
        normed = (center * lax.rsqrt(spread + 1e-05)).astype(BF)
        value = lax.dot_general(
            normed, fc1[...], (((1,), (1,)), ((), ())), preferred_element_type=F32
        )
        hidden = (0.5 * value * (1.0 + lax.erf(value * math.sqrt(0.5)))).astype(BF)
        return dot(hidden, fc2[...])

    send[...] = rows(1 - core[0]).astype(BF).reshape(send.shape)
    keep[...] = rows(core[0]).reshape(keep.shape)


def layer(core, tokens, fc1, fc2):
    dims = (NY, tokens.shape[0] // (NC * NY), tokens.shape[1])
    smem, vmem, anywhere = (
        pl.BlockSpec(memory_space=space) for space in (pltpu.SMEM, pltpu.VMEM, pl.ANY)
    )
    return pl.pallas_call(
        layer_body,
        in_specs=[smem] + [anywhere] * 3,
        out_specs=[vmem] * 2,
        out_shape=[shape(dims), shape(dims, F32)],
        scratch_shapes=[
            pltpu.VMEM(tokens.shape, BF),
            pltpu.VMEM(fc1.shape, BF),
            pltpu.VMEM(fc2.shape, BF),
            pltpu.SemaphoreType.DMA((12,)),
        ],
        compiler_params=pltpu.CompilerParams(vmem_limit_bytes=RELAY_LIMIT),
        cost_estimate=pl.CostEstimate(flops=COST, bytes_accessed=COST, transcendentals=0),
    )(core, tokens, fc1, fc2)


def regroup_body(shard, encoded, inter, out):
    part = encoded.shape[0] // 4
    for r in range(0, encoded.shape[0], part):
        features = jnp.concatenate([encoded[r : r + part], inter[r : r + part]], 1)
        for x in range(NX):
            for half in range(2):
                places = range(half * NZ // 2, (half + 1) * NZ // 2)
                starts = [(z * NX + x) * shard for z in places]
                out[2 * x + half, r : r + part] = jnp.concatenate(
                    [features[:, s : s + shard] for s in starts], 1
                )


def regroup(encoded, inter, shard):
    dims = (2 * NX, encoded.shape[0], NZ // 2 * shard)
    return call(functools.partial(regroup_body, shard), shape(dims), [], [encoded, inter])


def relay_body(tile_len, owners, encoded, inter, weight, hot, hidden, query, out, features, table, total, sems):
    split = encoded.shape[1]
    steps = weight.shape[0] // split
    copies = []
    for k in range(steps):
        rows = pl.ds(k * split, split)
        source = encoded if k == 0 else inter.at[:, pl.ds((k - 1) * split, split)]
        copies.append(pltpu.make_async_copy(source, features.at[k], sems.at[2 * k]))
        copies.append(pltpu.make_async_copy(weight.at[rows], table.at[k], sems.at[2 * k + 1]))
    for copy in copies:
        copy.start()
    out[:, :tile_len, :] = jnp.zeros((NIMG, tile_len, KVW), BF)

    slots = dot(hot[...], hidden[...]).astype(BF)
    for p in range(GROUP * HD // (2 * KVW)):
        pair = [
            dot(slots, query[:, (2 * p + i) * KVW : (2 * p + i + 1) * KVW]).reshape(
                NIMG, CAP, KVW
            )
            for i in range(2)
        ]
        start = tile_len + 2 * CAP * p
        out[:, start : start + 2 * CAP, :] = jnp.concatenate(pair, 1).astype(BF)

    for k in range(steps):
        copies[2 * k].wait()
        copies[2 * k + 1].wait()
        if k == 0:
            total[...] = dot(features[k], table[k])
        else:
            total[...] += dot(features[k], table[k])
    keys = rms_scale(total[:, :HD], 1e-06)
    tokens = jnp.concatenate([keys, total[:, HD:]], 1).astype(BF)
    for q in range(BLOCK):
        owner = owners[q]

        @pl.when(owner >= 0)
        def _(q=q, owner=owner):
            out[owner, :tile_len, :] = tokens[q * tile_len : (q + 1) * tile_len]


def relay_rows(owners, encoded, inter, weight, hot, hidden, query, after):
    rows, split = encoded.shape
    tile_len = rows // BLOCK
    height = tile_len + CAP * GROUP * HD // KVW
    steps = weight.shape[0] // split
    smem, vmem, hbm = (
        pl.BlockSpec(memory_space=space) for space in (pltpu.SMEM, pltpu.VMEM, pl.ANY)
    )

    def body(*refs):
        relay_body(tile_len, *refs[:7], *refs[7 + len(after) :])

    return pl.pallas_call(
        body,
        in_specs=[smem] + [hbm] * 3 + [vmem] * 3 + [hbm] * len(after),
        out_specs=vmem,
        out_shape=shape((NIMG, height, KVW)),
        scratch_shapes=[
            pltpu.VMEM((steps, rows, split), BF),
            pltpu.VMEM((steps, split, KVW), BF),
            pltpu.VMEM((rows, KVW), F32),
            pltpu.SemaphoreType.DMA((2 * steps,)),
        ],
        compiler_params=pltpu.CompilerParams(vmem_limit_bytes=RELAY_LIMIT),
        cost_estimate=pl.CostEstimate(flops=COST, bytes_accessed=COST, transcendentals=0),
    )(owners, encoded, inter, weight, hot, hidden, query, *after)


def decode_body(tile_len, info, arrived, cache, attended):
    groups = NIMG // TILES
    length = TILES * tile_len
    sums = jnp.sum(arrived[:, tile_len:, :].astype(F32), 0)
    queries = [
        rms_scale(sums[:, h * HD : (h + 1) * HD], 1e-06).reshape(-1, CAP, HD) for h in range(2)
    ]
    results = []
    for c in range(CAP):
        block, present, count = info[0, c], info[1, c] > 0, info[2, c]
        for j in range(TILES):
            rows = arrived[j * groups + block, :tile_len, :]
            cache[c, j * tile_len : (j + 1) * tile_len, :] = jnp.where(
                present, rows, jnp.zeros_like(rows)
            )
        keys, values = cache[c, :, :HD], cache[c, :, HD:]
        heads = jnp.concatenate([q[:, c, :] for q in queries], 0).astype(BF)
        scores = lax.dot_general(
            heads, keys, (((1,), (1,)), ((), ())), preferred_element_type=F32
        ) / math.sqrt(HD)
        tile = lax.broadcasted_iota(I32, (GROUP, length), 1) // tile_len
        weights = jnp.where(tile < count, jnp.exp(scores), 0.0).astype(BF)
        totals = jnp.sum(weights.astype(F32), -1, keepdims=True)
        result = dot(weights, values) / totals
        results.append(jnp.where(present, result, jnp.zeros_like(result)))
    for row in range(GROUP):
        head = row % (GROUP // 2) * 2 + row // (GROUP // 2)
        column = jnp.concatenate([r[row : row + 1] for r in results], 0)
        attended[:, head * HD : (head + 1) * HD] = column.astype(BF)


def decode(info, arrived, tile_len):
    outs = [shape((CAP, TILES * tile_len, KVW)), shape((CAP, GROUP * HD))]
    return call(functools.partial(decode_body, tile_len), outs, [info], [arrived])


def near_body(x, feats, own, left, right, out, across):
    for half in range(2):
        across[half] = feats[(x[0] + HOPS[-1]) % NX * 2 + half]
    mid = own.shape[0] // 2
    for step, weight in zip(HOPS, (own, left, right)):
        row = (x[0] + step) % NX * 2
        term = dot(feats[row], weight[:mid]) + dot(feats[row + 1], weight[mid:])
        if step == 0:
            out[...] = term
        else:
            out[...] += term


def near_sum(x, feats, weights):
    outs = [shape((feats.shape[1], weights[0].shape[1]), F32), shape((2,) + feats.shape[1:])]
    return call(near_body, outs, [x], [feats, *weights])


def last_body(near, across, first, second, out):
    total = dot(across[0], first[...]) + dot(across[1], second[...])
    out[...] = (near[...] + total).astype(BF)


def last_sum(near, across, far, after):
    return call(last_body, shape(near.shape), [], [near, across, *far], after, cost=LAST_COST)


def per_device(
    vision_tokens,
    inter_feats,
    fc1_weight,
    fc2_weight,
    proj_weight,
    kv_weight,
    tile_counts,
    owner_map,
    decode_hidden,
    query_weight,
):
    zi, xi = lax.axis_index("z"), lax.axis_index("x")
    yi, ci = lax.axis_index("y"), lax.axis_index("c")
    img_index = zi * NX + xi
    core = ci.astype(I32)[None]
    column = xi.astype(I32)[None]
    there = yi.astype(I32)[None]
    rows, width = vision_tokens.shape
    shard = proj_weight.shape[0]
    tile_len = rows // BLOCK
    requests = tile_counts.shape[0]

    late = lax.all_gather(proj_weight, "z", axis=0, tiled=True)
    left, right = shift(late, "x", 1), shift(late, "x", -1)
    mid = late.shape[0] // 2
    far = [shift(left[:mid], "x", 1), shift(right[mid:], "x", -1)]

    send, keep = layer(core, vision_tokens, fc1_weight.T, fc2_weight)
    swapped = shift(send, "c", 1)

    fold_send, fold_keep = fold_weights(core, proj_weight, kv_weight, [send])
    *fold_parts, fold_own = half_sums(there, shift(fold_send, "c", 1), fold_keep)
    fold_parts = [shift(p, "y", step) for step, p in zip((1, -1, 2), fold_parts)]

    request_ids = jnp.arange(requests, dtype=I32)
    same_owner = owner_map[:, None] == owner_map[None, :]
    earlier = same_owner & (request_ids[None, :] < request_ids[:, None])
    slot_rank = jnp.sum(earlier.astype(I32), 1)
    slot_match = (owner_map[None, :] == img_index) & (
        slot_rank[None, :] == jnp.arange(CAP, dtype=I32)[:, None]
    )
    present = jnp.any(slot_match, 1)
    request_of = jnp.sum(jnp.where(slot_match, request_ids[None, :], 0), 1)
    count_of = jnp.where(
        present, jnp.sum(jnp.where(slot_match, tile_counts[None, :], 0), 1), 1
    )
    info = jnp.stack([request_of // BLOCK, present.astype(I32), count_of])

    *parts, total = half_sums(there, swapped, keep)
    for step, part in zip((1, -1, 2), parts):
        total = total + shift(part, "y", step).astype(F32)
    quarter = rows // (NC * NY)
    tokens_here = pick(vision_tokens.reshape(NC * NY, quarter, width), ci * NY + yi)
    piece = (tokens_here.astype(F32) + total).astype(BF)
    gathered = [shift(piece, "y", step) for step in (1, -1, 2)]
    pieces = in_order(there, [piece, *gathered], []).reshape(rows // 2, width)
    encoded = pair(core, pieces, shift(pieces, "c", 1)).reshape(rows, width)

    joined = join(fold_own, fold_parts, [tick(v) for v in gathered])
    block = [joined, *(shift(joined, "x", step) for step in (1, -1, 2))]
    block = in_order(column, block, [tick(late)]).reshape(NX * shard, -1)
    early = lax.all_gather(block, "z", axis=0, tiled=True)

    slot_row = jnp.arange(NIMG * CAP, dtype=I32)
    slot_hot = (owner_map[None, :] == (slot_row // CAP)[:, None]) & (
        slot_rank[None, :] == (slot_row % CAP)[:, None]
    )
    feats = regroup(encoded, inter_feats, shard)
    tile_here, block_here = img_index // NZ, img_index % NZ
    owners_here = lax.dynamic_slice_in_dim(owner_map, block_here * BLOCK, BLOCK)
    counts_here = lax.dynamic_slice_in_dim(tile_counts, block_here * BLOCK, BLOCK)
    targets = jnp.where(tile_here < counts_here, owners_here, -1)
    outgoing = relay_rows(
        targets, encoded, inter_feats, early, slot_hot.astype(BF), decode_hidden, query_weight, [tick(feats)]
    )
    arrived = lax.all_to_all(outgoing, ("z", "x"), 0, 0, tiled=True)
    kv_cache, attended = decode(info, arrived, tile_len)

    near, across = near_sum(column, feats, [late, left, right])
    vision_states = last_sum(near, across, far, [])
    return (vision_states, kv_cache, attended)


def solution(mesh):
    img, tp = ("z", "x"), ("y", "c")
    fine = Mesh(mesh.devices.reshape(NZ, NX, NY, NC), img + tp)
    return jax.shard_map(
        per_device,
        mesh=fine,
        in_specs=(
            P(img, None),
            P(img, None),
            P(None, tp),
            P(tp, None),
            P(img, tp),
            P(tp, None),
            P(),
            P(),
            P(None, img),
            P(img, tp),
        ),
        out_specs=(P(img, tp), P(img, None, tp), P(img, tp)),
        check_vma=False,
    )
```

```python
import functools
import math

import jax
import jax.numpy as jnp
from jax import lax
from jax.experimental import pallas as pl
from jax.experimental.pallas import tpu as pltpu
from jax.sharding import Mesh, PartitionSpec as P

QH = 64
KVH = 8
HD = 128
TILES = 4
NZ, NX, NY, NC = 8, 4, 4, 2
NIMG = NZ * NX
BLOCK = 16
CAP = 8
GROUP = QH // KVH
KVW = 2 * HD
BF = jnp.bfloat16
F32 = jnp.float32
I32 = jnp.int32
VMEM_LIMIT = 14 * 2**20
COST = 1
LAST_COST = 10**9
RELAY_LIMIT = 56 * 2**20
HOPS = (0, -1, 1, 2)
HOPS = (0, -1, 1, 2)


def shift(value, axis, step):
    n = lax.axis_size(axis)
    return lax.ppermute(value, axis, [(i, (i + step) % n) for i in range(n)])


def tick(array):
    return array.reshape(-1, array.shape[-1])[:8, :HD]


def dot(a, b):
    return jnp.dot(a, b, preferred_element_type=F32)


def pick(array, index, axis=0):
    return lax.dynamic_index_in_dim(array, index, axis, keepdims=False)


def place(buffer, value, index, axis):
    return lax.dynamic_update_index_in_dim(buffer, value, index, axis)


def rms_scale(values, epsilon):
    return values * lax.rsqrt(jnp.mean(values * values, -1, keepdims=True) + epsilon)


def shape(dims, dtype=BF):
    return jax.ShapeDtypeStruct(dims, dtype)


def call(body, out_shape, scalars, operands, after=(), scratch=(), space=pltpu.VMEM, cost=COST):
    lead = len(scalars) + len(operands)

    def kernel(*refs):
        body(*refs[:lead], *refs[lead + len(after) :])

    smem, vmem = (pl.BlockSpec(memory_space=space) for space in (pltpu.SMEM, pltpu.VMEM))
    several = isinstance(out_shape, (list, tuple))
    return pl.pallas_call(
        kernel,
        in_specs=[smem] * len(scalars)
        + [pl.BlockSpec(memory_space=space)] * len(operands)
        + [pl.BlockSpec(memory_space=pl.ANY)] * len(after),
        out_specs=[vmem] * len(out_shape) if several else vmem,
        out_shape=out_shape,
        scratch_shapes=scratch,
        compiler_params=pltpu.CompilerParams(vmem_limit_bytes=VMEM_LIMIT),
        cost_estimate=pl.CostEstimate(flops=cost, bytes_accessed=cost, transcendentals=0),
    )(*scalars, *operands, *after)


def fold_body(core, proj, kv, send, keep):
    for here in range(NC):

        @pl.when(core[0] == here)
        def _(here=here):
            for y in range(NY):
                other, mine = (2 * y + 1 - here) * KVW, (2 * y + here) * KVW
                send[y] = dot(proj[...], kv[:, other : other + KVW]).astype(BF)
                keep[y] = dot(proj[...], kv[:, mine : mine + KVW])


def fold_weights(core, proj, kv, after):
    dims = (NY, proj.shape[0], KVW)
    return call(fold_body, [shape(dims), shape(dims, F32)], [core], [proj, kv], after)


def half_body(y, swapped, keep, up, down, across, own):
    for step, out in ((1, up), (NY - 1, down), (2, across)):
        place = (y[0] + step) % NY
        out[...] = (swapped[place].astype(F32) + keep[place]).astype(BF)
    own[...] = swapped[y[0]].astype(F32) + keep[y[0]]


def half_sums(y, swapped, keep, after=()):
    dims = keep.shape[1:]
    outs = [shape(dims)] * 3 + [shape(dims, F32)]
    return call(half_body, outs, [y], [swapped, keep], after)


def join_body(own, up, down, across, out):
    total = own[...] + up[...].astype(F32) + down[...].astype(F32) + across[...].astype(F32)
    out[...] = total.astype(BF)


def join(own, parts, after):
    return call(join_body, shape(own.shape), [], [own, *parts], after)


def block_body(x, own, left, right, far, out):
    for step, value in zip(HOPS, (own, left, right, far)):
        out[(x[0] + step) % NX] = value[...]


def pair_body(which, own, other, out):
    out[which[0]] = own[...]
    out[1 - which[0]] = other[...]


def pair(which, own, other):
    return call(pair_body, shape((NC,) + own.shape), [which], [own, other])


def in_order(x, parts, after):
    return call(block_body, shape((NX,) + parts[0].shape), [x], parts, after)


def layer_body(core, source, first, second, send, keep, tokens, fc1, fc2, sems):
    parts = 4
    pairs = []
    for ref, place in ((source, tokens), (first, fc1), (second, fc2)):
        rows = ref.shape[0] // parts
        pairs += [
            (ref.at[k * rows : (k + 1) * rows], place.at[k * rows : (k + 1) * rows])
            for k in range(parts)
        ]
    copies = [pltpu.make_async_copy(s, d, sems.at[i]) for i, (s, d) in enumerate(pairs)]
    for copy in copies:
        copy.start()
    for copy in copies:
        copy.wait()
    half = tokens.shape[0] // NC

    def rows(which):
        wide = tokens[pl.ds(pl.multiple_of(which * half, half), half), :].astype(F32)
        center = wide - jnp.mean(wide, -1, keepdims=True)
        spread = jnp.mean(center * center, -1, keepdims=True)
        normed = (center * lax.rsqrt(spread + 1e-05)).astype(BF)
        value = lax.dot_general(
            normed, fc1[...], (((1,), (1,)), ((), ())), preferred_element_type=F32
        )
        hidden = (0.5 * value * (1.0 + lax.erf(value * math.sqrt(0.5)))).astype(BF)
        return dot(hidden, fc2[...])

    send[...] = rows(1 - core[0]).astype(BF).reshape(send.shape)
    keep[...] = rows(core[0]).reshape(keep.shape)


def layer(core, tokens, fc1, fc2):
    dims = (NY, tokens.shape[0] // (NC * NY), tokens.shape[1])
    smem, vmem, anywhere = (
        pl.BlockSpec(memory_space=space) for space in (pltpu.SMEM, pltpu.VMEM, pl.ANY)
    )
    return pl.pallas_call(
        layer_body,
        in_specs=[smem] + [anywhere] * 3,
        out_specs=[vmem] * 2,
        out_shape=[shape(dims), shape(dims, F32)],
        scratch_shapes=[
            pltpu.VMEM(tokens.shape, BF),
            pltpu.VMEM(fc1.shape, BF),
            pltpu.VMEM(fc2.shape, BF),
            pltpu.SemaphoreType.DMA((12,)),
        ],
        compiler_params=pltpu.CompilerParams(vmem_limit_bytes=RELAY_LIMIT),
        cost_estimate=pl.CostEstimate(flops=COST, bytes_accessed=COST, transcendentals=0),
    )(core, tokens, fc1, fc2)


def regroup_body(shard, encoded, inter, out):
    part = encoded.shape[0] // 4
    for r in range(0, encoded.shape[0], part):
        features = jnp.concatenate([encoded[r : r + part], inter[r : r + part]], 1)
        for x in range(NX):
            for half in range(2):
                places = range(half * NZ // 2, (half + 1) * NZ // 2)
                starts = [(z * NX + x) * shard for z in places]
                out[2 * x + half, r : r + part] = jnp.concatenate(
                    [features[:, s : s + shard] for s in starts], 1
                )


def regroup(encoded, inter, shard):
    dims = (2 * NX, encoded.shape[0], NZ // 2 * shard)
    return call(functools.partial(regroup_body, shard), shape(dims), [], [encoded, inter])


def relay_body(tile_len, owners, encoded, inter, weight, hot, hidden, query, out, features, table, total, sems):
    split = encoded.shape[1]
    steps = weight.shape[0] // split
    copies = []
    for k in range(steps):
        for part in range(2):
            tall, deep = encoded.shape[0] // 2, split // 2
            rows = pl.ds(part * tall, tall)
            columns = pl.ds(0 if k == 0 else (k - 1) * split, split)
            source = (encoded if k == 0 else inter).at[rows, columns]
            here = weight.at[pl.ds(k * split + part * deep, deep)]
            there = table.at[k, pl.ds(part * deep, deep)]
            sem = 4 * k + 2 * part
            copies.append(pltpu.make_async_copy(source, features.at[k, rows], sems.at[sem]))
            copies.append(pltpu.make_async_copy(here, there, sems.at[sem + 1]))
    for copy in copies:
        copy.start()
    out[:, :tile_len, :] = jnp.zeros((NIMG, tile_len, KVW), BF)

    slots = dot(hot[...], hidden[...]).astype(BF)
    for p in range(GROUP * HD // (2 * KVW)):
        pair = [
            dot(slots, query[:, (2 * p + i) * KVW : (2 * p + i + 1) * KVW]).reshape(
                NIMG, CAP, KVW
            )
            for i in range(2)
        ]
        start = tile_len + 2 * CAP * p
        out[:, start : start + 2 * CAP, :] = jnp.concatenate(pair, 1).astype(BF)

    for k in range(steps):
        for copy in copies[4 * k : 4 * k + 4]:
            copy.wait()
        if k == 0:
            total[...] = dot(features[k], table[k])
        else:
            total[...] += dot(features[k], table[k])
    keys = rms_scale(total[:, :HD], 1e-06)
    tokens = jnp.concatenate([keys, total[:, HD:]], 1).astype(BF)
    for q in range(BLOCK):
        owner = owners[q]

        @pl.when(owner >= 0)
        def _(q=q, owner=owner):
            out[owner, :tile_len, :] = tokens[q * tile_len : (q + 1) * tile_len]


def relay_rows(owners, encoded, inter, weight, hot, hidden, query, after):
    rows, split = encoded.shape
    tile_len = rows // BLOCK
    height = tile_len + CAP * GROUP * HD // KVW
    steps = weight.shape[0] // split
    smem, vmem, hbm = (
        pl.BlockSpec(memory_space=space) for space in (pltpu.SMEM, pltpu.VMEM, pl.ANY)
    )

    def body(*refs):
        relay_body(tile_len, *refs[:7], *refs[7 + len(after) :])

    return pl.pallas_call(
        body,
        in_specs=[smem] + [hbm] * 3 + [vmem] * 3 + [hbm] * len(after),
        out_specs=vmem,
        out_shape=shape((NIMG, height, KVW)),
        scratch_shapes=[
            pltpu.VMEM((steps, rows, split), BF),
            pltpu.VMEM((steps, split, KVW), BF),
            pltpu.VMEM((rows, KVW), F32),
            pltpu.SemaphoreType.DMA((4 * steps,)),
        ],
        compiler_params=pltpu.CompilerParams(vmem_limit_bytes=RELAY_LIMIT),
        cost_estimate=pl.CostEstimate(flops=COST, bytes_accessed=COST, transcendentals=0),
    )(owners, encoded, inter, weight, hot, hidden, query, *after)


def decode_body(tile_len, info, arrived, cache, attended):
    groups = NIMG // TILES
    length = TILES * tile_len
    sums = jnp.sum(arrived[:, tile_len:, :].astype(F32), 0)
    queries = [
        rms_scale(sums[:, h * HD : (h + 1) * HD], 1e-06).reshape(-1, CAP, HD) for h in range(2)
    ]
    stored, lives = [], []
    for c in range(CAP):
        block, present = info[0, c], info[1, c] > 0
        rows = [arrived[j * groups + block, :tile_len, :] for j in range(TILES)]
        rows = jnp.concatenate(rows, 0)
        rows = jnp.where(present, rows, jnp.zeros_like(rows))
        cache[c] = rows
        stored.append(rows)
        lives.append(present)
    scores = []
    for c in range(CAP):
        heads = jnp.concatenate([q[:, c, :] for q in queries], 0).astype(BF)
        scores.append(
            lax.dot_general(
                heads, stored[c][:, :HD], (((1,), (1,)), ((), ())), preferred_element_type=F32
            )
            / math.sqrt(HD)
        )
    tile = lax.broadcasted_iota(I32, (GROUP, length), 1) // tile_len
    weights = [
        jnp.where(tile < info[2, c], jnp.exp(scores[c]), 0.0).astype(BF) for c in range(CAP)
    ]
    results = []
    for c in range(CAP):
        totals = jnp.sum(weights[c].astype(F32), -1, keepdims=True)
        result = dot(weights[c], stored[c][:, HD:]) / totals
        results.append(jnp.where(lives[c], result, jnp.zeros_like(result)))
    for row in range(GROUP):
        head = row % (GROUP // 2) * 2 + row // (GROUP // 2)
        column = jnp.concatenate([r[row : row + 1] for r in results], 0)
        attended[:, head * HD : (head + 1) * HD] = column.astype(BF)


def decode(info, arrived, tile_len):
    outs = [shape((CAP, TILES * tile_len, KVW)), shape((CAP, GROUP * HD))]
    return call(functools.partial(decode_body, tile_len), outs, [info], [arrived])


def near_body(x, feats, own, left, right, out, across):
    for half in range(2):
        across[half] = feats[(x[0] + HOPS[-1]) % NX * 2 + half]
    mid = own.shape[0] // 2
    for step, weight in zip(HOPS, (own, left, right)):
        row = (x[0] + step) % NX * 2
        term = dot(feats[row], weight[:mid]) + dot(feats[row + 1], weight[mid:])
        if step == 0:
            out[...] = term
        else:
            out[...] += term


def near_sum(x, feats, weights):
    outs = [shape((feats.shape[1], weights[0].shape[1]), F32), shape((2,) + feats.shape[1:])]
    return call(near_body, outs, [x], [feats, *weights])


def last_body(near, across, first, second, out):
    total = dot(across[0], first[...]) + dot(across[1], second[...])
    out[...] = (near[...] + total).astype(BF)


def last_sum(near, across, far, after):
    return call(last_body, shape(near.shape), [], [near, across, *far], after, cost=LAST_COST)


def per_device(
    vision_tokens,
    inter_feats,
    fc1_weight,
    fc2_weight,
    proj_weight,
    kv_weight,
    tile_counts,
    owner_map,
    decode_hidden,
    query_weight,
):
    zi, xi = lax.axis_index("z"), lax.axis_index("x")
    yi, ci = lax.axis_index("y"), lax.axis_index("c")
    img_index = zi * NX + xi
    core = ci.astype(I32)[None]
    column = xi.astype(I32)[None]
    there = yi.astype(I32)[None]
    rows, width = vision_tokens.shape
    shard = proj_weight.shape[0]
    tile_len = rows // BLOCK
    requests = tile_counts.shape[0]

    late = lax.all_gather(proj_weight, "z", axis=0, tiled=True)
    left, right = shift(late, "x", 1), shift(late, "x", -1)
    mid = late.shape[0] // 2
    far = [shift(left[:mid], "x", 1), shift(right[mid:], "x", -1)]

    send, keep = layer(core, vision_tokens, fc1_weight.T, fc2_weight)
    swapped = shift(send, "c", 1)

    fold_send, fold_keep = fold_weights(core, proj_weight, kv_weight, [send])
    *fold_parts, fold_own = half_sums(there, shift(fold_send, "c", 1), fold_keep)
    fold_parts = [shift(p, "y", step) for step, p in zip((1, -1, 2), fold_parts)]

    request_ids = jnp.arange(requests, dtype=I32)
    same_owner = owner_map[:, None] == owner_map[None, :]
    earlier = same_owner & (request_ids[None, :] < request_ids[:, None])
    slot_rank = jnp.sum(earlier.astype(I32), 1)
    slot_match = (owner_map[None, :] == img_index) & (
        slot_rank[None, :] == jnp.arange(CAP, dtype=I32)[:, None]
    )
    present = jnp.any(slot_match, 1)
    request_of = jnp.sum(jnp.where(slot_match, request_ids[None, :], 0), 1)
    count_of = jnp.where(
        present, jnp.sum(jnp.where(slot_match, tile_counts[None, :], 0), 1), 1
    )
    info = jnp.stack([request_of // BLOCK, present.astype(I32), count_of])

    *parts, total = half_sums(there, swapped, keep)
    for step, part in zip((1, -1, 2), parts):
        total = total + shift(part, "y", step).astype(F32)
    quarter = rows // (NC * NY)
    tokens_here = pick(vision_tokens.reshape(NC * NY, quarter, width), ci * NY + yi)
    piece = (tokens_here.astype(F32) + total).astype(BF)
    gathered = [shift(piece, "y", step) for step in (1, -1, 2)]
    pieces = in_order(there, [piece, *gathered], []).reshape(rows // 2, width)
    encoded = pair(core, pieces, shift(pieces, "c", 1)).reshape(rows, width)

    joined = join(fold_own, fold_parts, [tick(v) for v in gathered])
    block = [joined, *(shift(joined, "x", step) for step in (1, -1, 2))]
    block = in_order(column, block, [tick(late)]).reshape(NX * shard, -1)
    early = lax.all_gather(block, "z", axis=0, tiled=True)

    slot_row = jnp.arange(NIMG * CAP, dtype=I32)
    slot_hot = (owner_map[None, :] == (slot_row // CAP)[:, None]) & (
        slot_rank[None, :] == (slot_row % CAP)[:, None]
    )
    feats = regroup(encoded, inter_feats, shard)
    tile_here, block_here = img_index // NZ, img_index % NZ
    owners_here = lax.dynamic_slice_in_dim(owner_map, block_here * BLOCK, BLOCK)
    counts_here = lax.dynamic_slice_in_dim(tile_counts, block_here * BLOCK, BLOCK)
    targets = jnp.where(tile_here < counts_here, owners_here, -1)
    outgoing = relay_rows(
        targets, encoded, inter_feats, early, slot_hot.astype(BF), decode_hidden, query_weight, [tick(feats)]
    )
    arrived = lax.all_to_all(outgoing, ("z", "x"), 0, 0, tiled=True)
    kv_cache, attended = decode(info, arrived, tile_len)

    near, across = near_sum(column, feats, [late, left, right])
    vision_states = last_sum(near, across, far, [])
    return (vision_states, kv_cache, attended)


def solution(mesh):
    img, tp = ("z", "x"), ("y", "c")
    fine = Mesh(mesh.devices.reshape(NZ, NX, NY, NC), img + tp)
    return jax.shard_map(
        per_device,
        mesh=fine,
        in_specs=(
            P(img, None),
            P(img, None),
            P(None, tp),
            P(tp, None),
            P(img, tp),
            P(tp, None),
            P(),
            P(),
            P(None, img),
            P(img, tp),
        ),
        out_specs=(P(img, tp), P(img, None, tp), P(img, tp)),
        check_vma=False,
    )
```

```python
import functools
import math

import jax
import jax.numpy as jnp
from jax import lax
from jax.experimental import pallas as pl
from jax.experimental.pallas import tpu as pltpu
from jax.sharding import Mesh, PartitionSpec as P

QH = 64
KVH = 8
HD = 128
TILES = 4
NZ, NX, NY, NC = 8, 4, 4, 2
NIMG = NZ * NX
BLOCK = 16
CAP = 8
GROUP = QH // KVH
KVW = 2 * HD
BF = jnp.bfloat16
F32 = jnp.float32
I32 = jnp.int32
VMEM_LIMIT = 14 * 2**20
COST = 1
LAST_COST = 10**9
RELAY_LIMIT = 56 * 2**20
HOPS = (0, -1, 1, 2)
HOPS = (0, -1, 1, 2)


def shift(value, axis, step):
    n = lax.axis_size(axis)
    return lax.ppermute(value, axis, [(i, (i + step) % n) for i in range(n)])


def tick(array):
    return array.reshape(-1, array.shape[-1])[:8, :HD]


def dot(a, b):
    return jnp.dot(a, b, preferred_element_type=F32)


def pick(array, index, axis=0):
    return lax.dynamic_index_in_dim(array, index, axis, keepdims=False)


def place(buffer, value, index, axis):
    return lax.dynamic_update_index_in_dim(buffer, value, index, axis)


def rms_scale(values, epsilon):
    return values * lax.rsqrt(jnp.mean(values * values, -1, keepdims=True) + epsilon)


def shape(dims, dtype=BF):
    return jax.ShapeDtypeStruct(dims, dtype)


def call(body, out_shape, scalars, operands, after=(), scratch=(), space=pltpu.VMEM, cost=COST):
    lead = len(scalars) + len(operands)

    def kernel(*refs):
        body(*refs[:lead], *refs[lead + len(after) :])

    smem, vmem = (pl.BlockSpec(memory_space=space) for space in (pltpu.SMEM, pltpu.VMEM))
    several = isinstance(out_shape, (list, tuple))
    return pl.pallas_call(
        kernel,
        in_specs=[smem] * len(scalars)
        + [pl.BlockSpec(memory_space=space)] * len(operands)
        + [pl.BlockSpec(memory_space=pl.ANY)] * len(after),
        out_specs=[vmem] * len(out_shape) if several else vmem,
        out_shape=out_shape,
        scratch_shapes=scratch,
        compiler_params=pltpu.CompilerParams(vmem_limit_bytes=VMEM_LIMIT),
        cost_estimate=pl.CostEstimate(flops=cost, bytes_accessed=cost, transcendentals=0),
    )(*scalars, *operands, *after)


def fold_body(core, proj, kv, send, keep):
    for here in range(NC):

        @pl.when(core[0] == here)
        def _(here=here):
            for y in range(NY):
                other, mine = (2 * y + 1 - here) * KVW, (2 * y + here) * KVW
                send[y] = dot(proj[...], kv[:, other : other + KVW]).astype(BF)
                keep[y] = dot(proj[...], kv[:, mine : mine + KVW])


def fold_weights(core, proj, kv, after):
    dims = (NY, proj.shape[0], KVW)
    return call(fold_body, [shape(dims), shape(dims, F32)], [core], [proj, kv], after)


def half_body(y, swapped, keep, up, down, across, own):
    for step, out in ((1, up), (NY - 1, down), (2, across)):
        place = (y[0] + step) % NY
        out[...] = (swapped[place].astype(F32) + keep[place]).astype(BF)
    own[...] = swapped[y[0]].astype(F32) + keep[y[0]]


def half_sums(y, swapped, keep, after=()):
    dims = keep.shape[1:]
    outs = [shape(dims)] * 3 + [shape(dims, F32)]
    return call(half_body, outs, [y], [swapped, keep], after)


def join_body(own, up, down, across, out):
    total = own[...] + up[...].astype(F32) + down[...].astype(F32) + across[...].astype(F32)
    out[...] = total.astype(BF)


def join(own, parts, after):
    return call(join_body, shape(own.shape), [], [own, *parts], after)


def block_body(x, own, left, right, far, out):
    for step, value in zip(HOPS, (own, left, right, far)):
        out[(x[0] + step) % NX] = value[...]


def pair_body(which, own, other, out):
    out[which[0]] = own[...]
    out[1 - which[0]] = other[...]


def pair(which, own, other):
    return call(pair_body, shape((NC,) + own.shape), [which], [own, other])


def in_order(x, parts, after):
    return call(block_body, shape((NX,) + parts[0].shape), [x], parts, after)


def layer_body(core, source, first, second, send, keep, tokens, fc1, fc2, sems):
    parts = 4
    pairs = []
    for ref, place in ((source, tokens), (first, fc1), (second, fc2)):
        rows = ref.shape[0] // parts
        pairs += [
            (ref.at[k * rows : (k + 1) * rows], place.at[k * rows : (k + 1) * rows])
            for k in range(parts)
        ]
    copies = [pltpu.make_async_copy(s, d, sems.at[i]) for i, (s, d) in enumerate(pairs)]
    for copy in copies:
        copy.start()
    for copy in copies:
        copy.wait()
    half = tokens.shape[0] // NC

    def rows(which):
        wide = tokens[pl.ds(pl.multiple_of(which * half, half), half), :].astype(F32)
        center = wide - jnp.mean(wide, -1, keepdims=True)
        spread = jnp.mean(center * center, -1, keepdims=True)
        normed = (center * lax.rsqrt(spread + 1e-05)).astype(BF)
        value = lax.dot_general(
            normed, fc1[...], (((1,), (1,)), ((), ())), preferred_element_type=F32
        )
        hidden = (0.5 * value * (1.0 + lax.erf(value * math.sqrt(0.5)))).astype(BF)
        return dot(hidden, fc2[...])

    send[...] = rows(1 - core[0]).astype(BF).reshape(send.shape)
    keep[...] = rows(core[0]).reshape(keep.shape)


def layer(core, tokens, fc1, fc2):
    dims = (NY, tokens.shape[0] // (NC * NY), tokens.shape[1])
    smem, vmem, anywhere = (
        pl.BlockSpec(memory_space=space) for space in (pltpu.SMEM, pltpu.VMEM, pl.ANY)
    )
    return pl.pallas_call(
        layer_body,
        in_specs=[smem] + [anywhere] * 3,
        out_specs=[vmem] * 2,
        out_shape=[shape(dims), shape(dims, F32)],
        scratch_shapes=[
            pltpu.VMEM(tokens.shape, BF),
            pltpu.VMEM(fc1.shape, BF),
            pltpu.VMEM(fc2.shape, BF),
            pltpu.SemaphoreType.DMA((12,)),
        ],
        compiler_params=pltpu.CompilerParams(vmem_limit_bytes=RELAY_LIMIT),
        cost_estimate=pl.CostEstimate(flops=COST, bytes_accessed=COST, transcendentals=0),
    )(core, tokens, fc1, fc2)


def regroup_body(shard, encoded, inter, out):
    part = encoded.shape[0] // 4
    for r in range(0, encoded.shape[0], part):
        features = jnp.concatenate([encoded[r : r + part], inter[r : r + part]], 1)
        for x in range(NX):
            for half in range(2):
                places = range(half * NZ // 2, (half + 1) * NZ // 2)
                starts = [(z * NX + x) * shard for z in places]
                out[2 * x + half, r : r + part] = jnp.concatenate(
                    [features[:, s : s + shard] for s in starts], 1
                )


def regroup(encoded, inter, shard):
    dims = (2 * NX, encoded.shape[0], NZ // 2 * shard)
    return call(functools.partial(regroup_body, shard), shape(dims), [], [encoded, inter])


def relay_body(tile_len, owners, encoded, inter, weight, hot, hidden, query, out, features, table, total, sems):
    split = encoded.shape[1]
    steps = weight.shape[0] // split
    copies = []
    for k in range(steps):
        for part in range(2):
            tall, deep = encoded.shape[0] // 2, split // 2
            rows = pl.ds(part * tall, tall)
            columns = pl.ds(0 if k == 0 else (k - 1) * split, split)
            source = (encoded if k == 0 else inter).at[rows, columns]
            here = weight.at[pl.ds(k * split + part * deep, deep)]
            there = table.at[k, pl.ds(part * deep, deep)]
            sem = 4 * k + 2 * part
            copies.append(pltpu.make_async_copy(source, features.at[k, rows], sems.at[sem]))
            copies.append(pltpu.make_async_copy(here, there, sems.at[sem + 1]))
    for copy in copies:
        copy.start()
    out[:, :tile_len, :] = jnp.zeros((NIMG, tile_len, KVW), BF)

    slots = dot(hot[...], hidden[...]).astype(BF)
    for p in range(GROUP * HD // (2 * KVW)):
        pair = [
            dot(slots, query[:, (2 * p + i) * KVW : (2 * p + i + 1) * KVW]).reshape(
                NIMG, CAP, KVW
            )
            for i in range(2)
        ]
        start = tile_len + 2 * CAP * p
        out[:, start : start + 2 * CAP, :] = jnp.concatenate(pair, 1).astype(BF)

    for k in range(steps):
        for copy in copies[4 * k : 4 * k + 4]:
            copy.wait()
        if k == 0:
            total[...] = dot(features[k], table[k])
        else:
            total[...] += dot(features[k], table[k])
    keys = rms_scale(total[:, :HD], 1e-06)
    tokens = jnp.concatenate([keys, total[:, HD:]], 1).astype(BF)
    for q in range(BLOCK):
        owner = owners[q]

        @pl.when(owner >= 0)
        def _(q=q, owner=owner):
            out[owner, :tile_len, :] = tokens[q * tile_len : (q + 1) * tile_len]


def relay_rows(owners, encoded, inter, weight, hot, hidden, query, after):
    rows, split = encoded.shape
    tile_len = rows // BLOCK
    height = tile_len + CAP * GROUP * HD // KVW
    steps = weight.shape[0] // split
    smem, vmem, hbm = (
        pl.BlockSpec(memory_space=space) for space in (pltpu.SMEM, pltpu.VMEM, pl.ANY)
    )

    def body(*refs):
        relay_body(tile_len, *refs[:7], *refs[7 + len(after) :])

    return pl.pallas_call(
        body,
        in_specs=[smem] + [hbm] * 3 + [vmem] * 3 + [hbm] * len(after),
        out_specs=vmem,
        out_shape=shape((NIMG, height, KVW)),
        scratch_shapes=[
            pltpu.VMEM((steps, rows, split), BF),
            pltpu.VMEM((steps, split, KVW), BF),
            pltpu.VMEM((rows, KVW), F32),
            pltpu.SemaphoreType.DMA((4 * steps,)),
        ],
        compiler_params=pltpu.CompilerParams(vmem_limit_bytes=RELAY_LIMIT),
        cost_estimate=pl.CostEstimate(flops=COST, bytes_accessed=COST, transcendentals=0),
    )(owners, encoded, inter, weight, hot, hidden, query, *after)


def decode_body(tile_len, info, arrived, cache, attended):
    groups = NIMG // TILES
    length = TILES * tile_len
    sums = jnp.sum(arrived[:, tile_len:, :].astype(F32), 0)
    queries = [
        rms_scale(sums[:, h * HD : (h + 1) * HD], 1e-06).reshape(-1, CAP, HD) for h in range(2)
    ]
    stored, lives = [], []
    for c in range(CAP):
        block, present = info[0, c], info[1, c] > 0
        rows = [arrived[j * groups + block, :tile_len, :] for j in range(TILES)]
        rows = jnp.concatenate(rows, 0)
        rows = jnp.where(present, rows, jnp.zeros_like(rows))
        cache[c] = rows
        stored.append(rows)
        lives.append(present)
    scores = []
    for c in range(CAP):
        heads = jnp.concatenate([q[:, c, :] for q in queries], 0).astype(BF)
        scores.append(
            lax.dot_general(
                heads, stored[c][:, :HD], (((1,), (1,)), ((), ())), preferred_element_type=F32
            )
            / math.sqrt(HD)
        )
    tile = lax.broadcasted_iota(I32, (GROUP, length), 1) // tile_len
    weights = [
        jnp.where(tile < info[2, c], jnp.exp(scores[c]), 0.0).astype(BF) for c in range(CAP)
    ]
    results = []
    for c in range(CAP):
        totals = jnp.sum(weights[c].astype(F32), -1, keepdims=True)
        result = dot(weights[c], stored[c][:, HD:]) / totals
        results.append(jnp.where(lives[c], result, jnp.zeros_like(result)))
    for row in range(GROUP):
        head = row % (GROUP // 2) * 2 + row // (GROUP // 2)
        column = jnp.concatenate([r[row : row + 1] for r in results], 0)
        attended[:, head * HD : (head + 1) * HD] = column.astype(BF)


def decode(info, arrived, tile_len):
    outs = [shape((CAP, TILES * tile_len, KVW)), shape((CAP, GROUP * HD))]
    return call(functools.partial(decode_body, tile_len), outs, [info], [arrived])


def near_body(x, feats, own, left, right, out, across):
    for half in range(2):
        across[half] = feats[(x[0] + HOPS[-1]) % NX * 2 + half]
    mid = own.shape[0] // 2
    for step, weight in zip(HOPS, (own, left, right)):
        row = (x[0] + step) % NX * 2
        term = dot(feats[row], weight[:mid]) + dot(feats[row + 1], weight[mid:])
        if step == 0:
            out[...] = term
        else:
            out[...] += term


def near_sum(x, feats, weights):
    outs = [shape((feats.shape[1], weights[0].shape[1]), F32), shape((2,) + feats.shape[1:])]
    return call(near_body, outs, [x], [feats, *weights])


def last_body(near, across, first, second, out, places, total, done, sems):
    copies = [
        pltpu.make_async_copy(w, places.at[k], sems.at[k]) for k, w in enumerate((first, second))
    ]
    for copy in copies:
        copy.start()
    copies[0].wait()
    total[...] = near[...] + dot(across[0], places[0])
    copies[1].wait()
    width = done.shape[1] // 2
    writes = []
    for k in range(2):
        columns = slice(k * width, (k + 1) * width)
        term = dot(across[1], places[1, :, columns])
        done[:, columns] = (total[:, columns] + term).astype(BF)
        writes.append(
            pltpu.make_async_copy(done.at[:, columns], out.at[:, columns], sems.at[2 + k])
        )
        writes[k].start()
    for write in writes:
        write.wait()


def last_sum(near, across, far):
    vmem, anywhere = (pl.BlockSpec(memory_space=space) for space in (pltpu.VMEM, pl.ANY))
    return pl.pallas_call(
        last_body,
        in_specs=[vmem] * 2 + [anywhere] * 2,
        out_specs=anywhere,
        out_shape=shape(near.shape),
        scratch_shapes=[
            pltpu.VMEM((2,) + far[0].shape, BF),
            pltpu.VMEM(near.shape, F32),
            pltpu.VMEM(near.shape, BF),
            pltpu.SemaphoreType.DMA((4,)),
        ],
        compiler_params=pltpu.CompilerParams(vmem_limit_bytes=VMEM_LIMIT),
        cost_estimate=pl.CostEstimate(
            flops=LAST_COST, bytes_accessed=LAST_COST, transcendentals=0
        ),
    )(near, across, *far)


def per_device(
    vision_tokens,
    inter_feats,
    fc1_weight,
    fc2_weight,
    proj_weight,
    kv_weight,
    tile_counts,
    owner_map,
    decode_hidden,
    query_weight,
):
    zi, xi = lax.axis_index("z"), lax.axis_index("x")
    yi, ci = lax.axis_index("y"), lax.axis_index("c")
    img_index = zi * NX + xi
    core = ci.astype(I32)[None]
    column = xi.astype(I32)[None]
    there = yi.astype(I32)[None]
    rows, width = vision_tokens.shape
    shard = proj_weight.shape[0]
    tile_len = rows // BLOCK
    requests = tile_counts.shape[0]

    late = lax.all_gather(proj_weight, "z", axis=0, tiled=True)
    left, right = shift(late, "x", 1), shift(late, "x", -1)
    mid = late.shape[0] // 2
    far = [shift(left[:mid], "x", 1), shift(right[mid:], "x", -1)]

    send, keep = layer(core, vision_tokens, fc1_weight.T, fc2_weight)
    swapped = shift(send, "c", 1)

    fold_send, fold_keep = fold_weights(core, proj_weight, kv_weight, [send])
    *fold_parts, fold_own = half_sums(there, shift(fold_send, "c", 1), fold_keep)
    fold_parts = [shift(p, "y", step) for step, p in zip((1, -1, 2), fold_parts)]

    request_ids = jnp.arange(requests, dtype=I32)
    same_owner = owner_map[:, None] == owner_map[None, :]
    earlier = same_owner & (request_ids[None, :] < request_ids[:, None])
    slot_rank = jnp.sum(earlier.astype(I32), 1)
    slot_match = (owner_map[None, :] == img_index) & (
        slot_rank[None, :] == jnp.arange(CAP, dtype=I32)[:, None]
    )
    present = jnp.any(slot_match, 1)
    request_of = jnp.sum(jnp.where(slot_match, request_ids[None, :], 0), 1)
    count_of = jnp.where(
        present, jnp.sum(jnp.where(slot_match, tile_counts[None, :], 0), 1), 1
    )
    info = jnp.stack([request_of // BLOCK, present.astype(I32), count_of])

    *parts, total = half_sums(there, swapped, keep)
    for step, part in zip((1, -1, 2), parts):
        total = total + shift(part, "y", step).astype(F32)
    quarter = rows // (NC * NY)
    tokens_here = pick(vision_tokens.reshape(NC * NY, quarter, width), ci * NY + yi)
    piece = (tokens_here.astype(F32) + total).astype(BF)
    gathered = [shift(piece, "y", step) for step in (1, -1, 2)]
    pieces = in_order(there, [piece, *gathered], []).reshape(rows // 2, width)
    encoded = pair(core, pieces, shift(pieces, "c", 1)).reshape(rows, width)

    joined = join(fold_own, fold_parts, [tick(v) for v in gathered])
    block = [joined, *(shift(joined, "x", step) for step in (1, -1, 2))]
    block = in_order(column, block, [tick(late)]).reshape(NX * shard, -1)
    early = lax.all_gather(block, "z", axis=0, tiled=True)

    slot_row = jnp.arange(NIMG * CAP, dtype=I32)
    slot_hot = (owner_map[None, :] == (slot_row // CAP)[:, None]) & (
        slot_rank[None, :] == (slot_row % CAP)[:, None]
    )
    feats = regroup(encoded, inter_feats, shard)
    tile_here, block_here = img_index // NZ, img_index % NZ
    owners_here = lax.dynamic_slice_in_dim(owner_map, block_here * BLOCK, BLOCK)
    counts_here = lax.dynamic_slice_in_dim(tile_counts, block_here * BLOCK, BLOCK)
    targets = jnp.where(tile_here < counts_here, owners_here, -1)
    outgoing = relay_rows(
        targets, encoded, inter_feats, early, slot_hot.astype(BF), decode_hidden, query_weight, [tick(feats)]
    )
    arrived = lax.all_to_all(outgoing, ("z", "x"), 0, 0, tiled=True)
    kv_cache, attended = decode(info, arrived, tile_len)

    near, across = near_sum(column, feats, [late, left, right])
    vision_states = last_sum(near, across, far)
    return (vision_states, kv_cache, attended)


def solution(mesh):
    img, tp = ("z", "x"), ("y", "c")
    fine = Mesh(mesh.devices.reshape(NZ, NX, NY, NC), img + tp)
    return jax.shard_map(
        per_device,
        mesh=fine,
        in_specs=(
            P(img, None),
            P(img, None),
            P(None, tp),
            P(tp, None),
            P(img, tp),
            P(tp, None),
            P(),
            P(),
            P(None, img),
            P(img, tp),
        ),
        out_specs=(P(img, tp), P(img, None, tp), P(img, tp)),
        check_vma=False,
    )
```
